128 devices in a mesh: ctx: 16 (over z, y_hi, core), exp: 8 (over y_lo, x).
Axes of the slice: x: 4, y: 4 (y_hi: 2, y_lo: 2; y = y_hi * 2 + y_lo), z: 4, core: 2. Of those that a mesh axis runs over, the one named last changes fastest.
Arguments:
- tokens: bfloat16 [2048, 2, 4096], P(('ctx', 'exp')), may hold values from -45 to 45
- queries: bfloat16 [2048, 2, 4096], P('ctx', None, 'exp'), may hold values from -7.5 to 7.5
- keys: bfloat16 [2048, 2, 256], P('ctx'), may hold values from -7.5 to 7.5
- values: bfloat16 [2048, 2, 256], P('ctx'), may hold values from -6 to 6
- output_weight: bfloat16 [4096, 4096], P('exp'), may hold values from -0.09375 to 0.09375
- norm_gain: bfloat16 [4096], replicated, may hold values from 0.25 to 1.75
- routing: int32 [2048, 2, 8], P(('ctx', 'exp')), may hold values from 0 to 127, all different within a row; in each aligned block of 32 rows (0 to 31, 32 to 63, ..., all dimensions but the last counted through in order) at most 3 rows name the same one
- gate_values: float32 [2048, 2, 8], P(('ctx', 'exp')), may hold values from 0.05 to 0.5
- expand_weight: bfloat16 [128, 4096, 1536], P(('ctx', 'exp')), may hold values from -0.09375 to 0.09375
- reduce_weight: bfloat16 [128, 768, 4096], P(('ctx', 'exp')), may hold values from -0.21875 to 0.21875
Outputs:
- layer_out: bfloat16 [2048, 2, 4096], P(('ctx', 'exp'))
The draws below stay inside these ranges and needn't reach their ends.
Inputs may be any that keep to these rules, and one draw needn't show every extreme that they name: `routing`: in each aligned block of 32 rows (position-major, both sequences of a position together) no expert is named by more than 3 rows, a bound that some block reaches.
All inputs are finite; a program needn't handle non-finite values.
Results may differ from the reference program's by a relative error of at most 0.015.
Values may be sent and summed in bfloat16 or wider, within the bound.
No kernel may reach another device: no remote copies, remote signals or barrier semaphores. Data moves between devices by JAX's collectives and lax.ppermute only.
A program may use at most 128 MiB of HBM per device.

```python
import math
import jax
import jax.numpy as jnp
import numpy as np
from jax import lax

D = 4096
HEADS = 32
KV_HEADS = 2
HEAD_DIM = 128
EW = 768
TOP = 8
PAIR = 2
SEQ = 2048
EXPERTS = 128
ROWS = 32
CAP = 3
N_CTX = 16
N_EXP = 8


def draw_queries(key, part):
    key = jax.random.fold_in(key, 11)
    result = jnp.clip(jax.random.normal(key, (SEQ, PAIR, HEADS * HEAD_DIM), jnp.float32), -5.0, 5.0) * 1.5
    return result.astype(jnp.bfloat16)


def draw_keys(key, part):
    key = jax.random.fold_in(key, 12)
    result = jnp.clip(jax.random.normal(key, (SEQ, PAIR, KV_HEADS * HEAD_DIM), jnp.float32), -5.0, 5.0) * 1.5
    return result.astype(jnp.bfloat16)


def draw_tokens(key, part):
    key = jax.random.fold_in(key, 13)
    row_key, column_key, entry_key = jax.random.split(key, 3)
    row_scale = jnp.exp(jax.random.uniform(row_key, (SEQ, PAIR, 1), jnp.float32, jnp.log(0.3), jnp.log(3.0)))
    column_scale = jnp.exp(jax.random.uniform(column_key, (D,), jnp.float32, jnp.log(0.3), jnp.log(3.0)))
    base = jnp.clip(jax.random.normal(entry_key, (SEQ, PAIR, D), jnp.float32), -5.0, 5.0)
    return (base * row_scale * column_scale[None, None, :]).astype(jnp.bfloat16)


def block_scale(stream_key, extent, pieces, low, largest):
    level, own = 1.0, jax.random.fold_in(stream_key, 6)
    for dim, shards_of in pieces:
        steps = jnp.exp(jax.random.uniform(jax.random.fold_in(own, dim), (shards_of,), jnp.float32, low / len(pieces), largest / len(pieces)))
        level = level * jnp.repeat(steps, extent[dim] // shards_of).reshape([-1 if axis == dim else 1 for axis in range(len(extent))])
    return level


def shared_out(rng, own, number, rows, amount, top, bound, lean):
    order = jax.random.permutation(rng, amount)
    heavy_load, common = load_shares(amount, rows * top, bound, lean, True), load_shares(amount, rows * top, bound, lean, False)
    places = jnp.arange(amount)

    def named(sizes, rotation):
        used = int((sizes > 0).sum())
        fixed = max(1, used // 4)
        shifted = fixed + (places - fixed + rotation * (used - fixed)) % max(1, amount - fixed)
        return jnp.zeros((amount,), jnp.int32).at[order[jnp.where(places < fixed, places, shifted)]].set(jnp.asarray(sizes, jnp.int32))

    sizes = jnp.where(number % 4 == 0, named(heavy_load, number // 4), named(common, number - number // 4 - 1))
    mixed = jax.random.permutation(jax.random.fold_in(own, 3), amount)
    donor, receiver = mixed[0:amount // 2 * 2:2], mixed[1:amount // 2 * 2:2]
    slack = jnp.minimum(sizes[donor] - 1, bound - sizes[receiver]) // 2
    slack = jnp.where((donor == order[0]) | (receiver == order[0]) | (sizes[receiver] == 0), 0, jnp.maximum(slack, 0))
    shifted = jax.random.randint(jax.random.fold_in(own, 4), (amount // 2,), 0, 1 << 20) % (slack + 1)
    sizes = sizes.at[donor].add(-shifted).at[receiver].add(shifted)
    members = jnp.searchsorted(jnp.cumsum(sizes), jnp.arange(rows * top), side="right").astype(jnp.int32)
    grid = members.reshape(top, rows).T
    grid = grid[jax.random.permutation(jax.random.fold_in(own, 1), rows)]
    rotation = jax.random.randint(jax.random.fold_in(own, 2), (rows, 1), 0, top)
    return jnp.take_along_axis(grid, (jnp.arange(top)[None, :] + rotation) % top, axis=1)


def load_shares(number_of, total, reach, skew, full):
    portions = [(1 << 20) // math.isqrt(standing ** skew) + 1 for standing in range(1, number_of + 1)]
    largest = reach if full else min(reach, max(-(-total // number_of), total * portions[0] // sum(portions)))
    least = 1 if total - largest >= number_of - 1 else 0
    counts, surplus = [largest] + [least] * (number_of - 1), total - largest - least * (number_of - 1)
    while surplus > 0:
        free = [i for i in range(1, number_of) if counts[i] < largest] or [i for i in range(1, number_of) if counts[i] < reach]
        mass, remaining = sum([portions[i] for i in free]), surplus
        for i in free:
            addition = min(reach - counts[i], max(1, remaining * portions[i] // mass), surplus)
            counts[i] = counts[i] + addition
            surplus = surplus - addition
    return np.array(counts)


def centred(stream_key, extent, scale, bound, shards=(), held_as=jnp.bfloat16):
    values = scale * jax.random.normal(stream_key, extent, jnp.float32)
    if shards:
        values = values * block_scale(stream_key, extent, shards, -0.22, 0.18)
    return jnp.clip(values, -bound, bound).astype(held_as)


def setup_inputs(seed: int = 0) -> dict:
    seeds = jax.random.split(jax.random.key(seed), 11)
    tokens = draw_tokens(jax.random.fold_in(seeds[10], 71), 0)
    queries = draw_queries(jax.random.fold_in(seeds[10], 71), 0)
    keys = draw_keys(jax.random.fold_in(seeds[10], 71), 0)
    values = centred(seeds[3], (SEQ, PAIR, KV_HEADS * HEAD_DIM), 1.0, 6.0, ((0, 16),))
    output_weight = centred(seeds[4], (HEADS * HEAD_DIM, D), (HEADS * HEAD_DIM) ** -0.5, 0.09375, ((0, 8),))
    norm_gain = jnp.clip(1.0 + 0.15 * jax.random.normal(seeds[5], (D,), jnp.float32), 0.25, 1.75).astype(jnp.bfloat16)
    routing_keys = jax.random.split(jax.random.fold_in(seeds[6], 1), SEQ * PAIR // ROWS)
    routing_turns = jax.random.permutation(jax.random.fold_in(seeds[6], 3), SEQ * PAIR // ROWS)
    routing = jax.vmap(lambda own, number: shared_out(jax.random.fold_in(seeds[6], 2), own, number, ROWS, EXPERTS, TOP, CAP, 1))(routing_keys, routing_turns).reshape((SEQ, PAIR, TOP))
    gate_values = jnp.clip(jnp.exp(math.log(0.5) - 2.3025851 * jax.random.uniform(seeds[7], (SEQ, PAIR, TOP), jnp.float32) ** block_scale(seeds[7], (SEQ, PAIR, TOP), ((0, 128),), -0.2, 0.2)), 0.05, 0.5)
    expand_weight = centred(seeds[8], (EXPERTS, D, 2 * EW), D ** -0.5, 0.09375, ((0, 128),))
    reduce_weight = centred(seeds[9], (EXPERTS, EW, D), EW ** -0.5, 0.21875, ((0, 128),))
    return dict(tokens=tokens, queries=queries, keys=keys, values=values, output_weight=output_weight, norm_gain=norm_gain, routing=routing, gate_values=gate_values, expand_weight=expand_weight, reduce_weight=reduce_weight)


def reference(tokens, queries, keys, values, output_weight, norm_gain, routing, gate_values, expand_weight, reduce_weight):
    head_group = HEADS // KV_HEADS
    score_scale = HEAD_DIM ** (-0.5)
    query_heads = jnp.transpose(queries.reshape(SEQ, PAIR, HEADS, HEAD_DIM), (1, 2, 0, 3)).reshape(PAIR * HEADS, SEQ, HEAD_DIM)
    key_heads = jnp.repeat(jnp.transpose(keys.reshape(SEQ, PAIR, KV_HEADS, HEAD_DIM), (1, 2, 0, 3)), head_group, axis=1).reshape(PAIR * HEADS, SEQ, HEAD_DIM)
    value_heads = jnp.repeat(jnp.transpose(values.reshape(SEQ, PAIR, KV_HEADS, HEAD_DIM), (1, 2, 0, 3)), head_group, axis=1).reshape(PAIR * HEADS, SEQ, HEAD_DIM)
    allowed = jnp.arange(SEQ)[None, :] <= jnp.arange(SEQ)[:, None]

    def attend_head(operands):
        query_rows, key_rows, value_rows = operands
        scores = jnp.dot(query_rows, key_rows.T, preferred_element_type=jnp.float32) * score_scale
        scores = jnp.where(allowed, scores, -1e+30)
        row_max = lax.optimization_barrier(jnp.max(scores, axis=1, keepdims=True))
        weights = jnp.where(allowed, jnp.exp(scores - row_max), 0.0)
        rounded = weights.astype(jnp.bfloat16)
        summed = jnp.dot(rounded, value_rows, preferred_element_type=jnp.float32)
        return (summed / lax.optimization_barrier(jnp.sum(weights, axis=1, keepdims=True))).astype(jnp.bfloat16)
    attended = lax.map(attend_head, (query_heads, key_heads, value_heads))
    attended = jnp.transpose(attended.reshape(PAIR, HEADS, SEQ, HEAD_DIM), (2, 0, 1, 3)).reshape(SEQ * PAIR, HEADS * HEAD_DIM)
    projected = jnp.dot(attended, output_weight, preferred_element_type=jnp.float32)
    stream = (tokens.reshape(SEQ * PAIR, D).astype(jnp.float32) + projected).astype(jnp.bfloat16)
    stream_wide = stream.astype(jnp.float32)
    normed = (stream_wide * lax.rsqrt(lax.optimization_barrier(jnp.mean(stream_wide * stream_wide, axis=1, keepdims=True)) + 1e-06) * norm_gain.astype(jnp.float32)).astype(jnp.bfloat16)
    flat_ids = routing.reshape(-1)
    flat_gates = gate_values.reshape(-1)
    limit = N_CTX * N_EXP * CAP

    def expert_step(mixture, operands):
        expert, inward, outward = operands
        hits = flat_ids == expert
        chosen = jnp.nonzero(hits, size=limit, fill_value=0)[0].astype(jnp.int32)
        live = jnp.arange(limit) < jnp.sum(hits.astype(jnp.int32))
        token_rows = chosen // TOP
        gated = jnp.dot(normed[token_rows], inward, preferred_element_type=jnp.float32)
        activated = (jax.nn.silu(gated[:, :EW]) * gated[:, EW:]).astype(jnp.bfloat16)
        expert_out = jnp.dot(activated, outward, preferred_element_type=jnp.float32).astype(jnp.bfloat16)
        weight = jnp.where(live, flat_gates[chosen], 0.0)
        return (mixture.at[token_rows].add(weight[:, None] * expert_out.astype(jnp.float32)), None)
    mixture, unused = lax.scan(expert_step, jnp.zeros((SEQ * PAIR, D), jnp.float32), (jnp.arange(EXPERTS, dtype=jnp.int32), expand_weight, reduce_weight))
    layer_out = (stream_wide + mixture).astype(jnp.bfloat16)
    return layer_out.reshape(SEQ, PAIR, D)
```

```python
import functools

import jax
import jax.numpy as jnp
from jax import lax
from jax.experimental import pallas as pl
from jax.experimental.pallas import tpu as pltpu
from jax.sharding import PartitionSpec as P

D = 4096
HEADS = 32
KV_HEADS = 2
HEAD_DIM = 128
EW = 768
TOP = 8
CAP = 3
PARTS = 8
PART = D // PARTS
LOG2E = 1.4426950408889634
F32 = jnp.float32
BF16 = jnp.bfloat16
MIB = 1 << 20


def contract(lhs, rhs, lhs_dim, rhs_dim):
    return lax.dot_general(
        lhs, rhs, (((lhs_dim,), (rhs_dim,)), ((), ())), preferred_element_type=F32
    )


def attend_kernel(pos_ref, q_ref, kv0_ref, kv1_ref, w_ref, out_ref, score_ref, *, blocks, length, pairs, heads):
    cols = heads * length
    query_pos = pos_ref[0] + lax.broadcasted_iota(jnp.int32, (length, cols), 1) % length
    key_iota = lax.broadcasted_iota(jnp.int32, (length, cols), 0)
    scale = HEAD_DIM ** (-0.5) * LOG2E
    total = 2 * blocks
    for p in range(pairs):
        query = jnp.concatenate(
            [
                q_ref[:, (p * heads + h) * HEAD_DIM : (p * heads + h + 1) * HEAD_DIM]
                for h in range(heads)
            ],
            axis=0,
        )
        top = jnp.full((1, cols), -1e30, F32)
        for b in range(total):
            source = kv0_ref if b < blocks else kv1_ref
            key = source[b % blocks, :, p * 2 * HEAD_DIM : (p * 2 + 1) * HEAD_DIM]
            score = contract(key, query, 1, 1) * scale
            score = jnp.where(key_iota + pos_ref[1 + b] <= query_pos, score, -1e30)
            score_ref[b] = score
            top = jnp.maximum(top, jnp.max(score, axis=0, keepdims=True))
        mass = jnp.zeros((1, cols), F32)
        acc = jnp.zeros((HEAD_DIM, cols), F32)
        for b in range(total):
            source = kv0_ref if b < blocks else kv1_ref
            value = source[b % blocks, :, (p * 2 + 1) * HEAD_DIM : (p * 2 + 2) * HEAD_DIM]
            weight = jnp.exp2(score_ref[b] - top)
            mass = mass + jnp.sum(weight, axis=0, keepdims=True)
            acc = acc + contract(value, weight.astype(BF16), 0, 0)
        attended = acc / mass
        attended = jnp.concatenate(
            [attended[:, h * length : (h + 1) * length].T for h in range(heads)], axis=1
        ).astype(BF16)
        groups = out_ref.shape[0]
        rows = length // groups
        step = 1024
        for n in range(0, D, step):
            part = jnp.dot(attended, w_ref[:, n : n + step], preferred_element_type=F32)
            out_ref[:, p * rows : (p + 1) * rows, n : n + step] = part.astype(BF16).reshape(
                groups, rows, step
            )


def prepare_kernel(routing_ref, gate_ref, place_ref, mix_ref):
    rows = routing_ref.shape[0]
    experts = place_ref.shape[0] // (CAP * PARTS)
    slots = place_ref.shape[0]
    width = PARTS * rows
    expert_iota = lax.broadcasted_iota(jnp.int32, (rows, experts), 1)
    named = jnp.zeros((rows, experts), F32)
    gates = jnp.zeros((rows, experts), F32)
    for k in range(TOP):
        hit = routing_ref[:, k : k + 1] == expert_iota
        named = jnp.where(hit, 1.0, named)
        gates = jnp.where(hit, gate_ref[:, k : k + 1], gates)
    lower = (
        lax.broadcasted_iota(jnp.int32, (rows, rows), 0)
        >= lax.broadcasted_iota(jnp.int32, (rows, rows), 1)
    ).astype(BF16)
    rank = named * jnp.dot(lower, named.astype(BF16), preferred_element_type=F32)
    spread = (
        lax.broadcasted_iota(jnp.int32, (rows, width), 0)
        == lax.broadcasted_iota(jnp.int32, (rows, width), 1) % rows
    ).astype(BF16)
    wide = contract(rank.astype(BF16), spread, 0, 0).astype(BF16)
    chunk = 768
    for s in range(0, slots, chunk):
        slot = s + lax.broadcasted_iota(jnp.int32, (chunk, experts), 0)
        owner = (
            slot // (CAP * PARTS) == lax.broadcasted_iota(jnp.int32, (chunk, experts), 1)
        ).astype(BF16)
        ranks = jnp.dot(owner, wide, preferred_element_type=F32)
        row = s + lax.broadcasted_iota(jnp.int32, (chunk, width), 0)
        col = lax.broadcasted_iota(jnp.int32, (chunk, width), 1)
        hit = (ranks == (row // PARTS % CAP + 1).astype(F32)) & (row % PARTS == col // rows)
        place_ref[s : s + chunk, :] = hit.astype(BF16)
        slot = s + lax.broadcasted_iota(jnp.int32, (experts, chunk), 1)
        owner = (
            slot // (CAP * PARTS) == lax.broadcasted_iota(jnp.int32, (experts, chunk), 0)
        ).astype(BF16)
        ranks = jnp.dot(rank.astype(BF16), owner, preferred_element_type=F32)
        value = jnp.dot(gates.astype(BF16), owner, preferred_element_type=F32)
        col = s + lax.broadcasted_iota(jnp.int32, (rows, chunk), 1)
        value = jnp.where(ranks == (col // PARTS % CAP + 1).astype(F32), value, 0.0)
        for c in range(PARTS):
            mix_ref[c * rows : (c + 1) * rows, s : s + chunk] = jnp.where(
                col % PARTS == c, value, 0.0
            ).astype(BF16)


def dispatch_kernel(part_ref, token_ref, gain_ref, place_ref, out_ref, stream_ref):
    sources = part_ref.shape[0]
    rows = token_ref.shape[0]
    square = jnp.zeros((rows, 1), F32)
    for c in range(PARTS):
        cols = slice(c * PART, (c + 1) * PART)
        total = part_ref[0, :, cols].astype(F32)
        for s in range(1, sources):
            total = total + part_ref[s, :, cols].astype(F32)
        stream = (token_ref[:, cols].astype(F32) + total).astype(BF16)
        stream_ref[c * rows : (c + 1) * rows, :] = stream
        wide = stream.astype(F32)
        square = square + jnp.sum(wide * wide, axis=1, keepdims=True)
    factor = lax.rsqrt(square * (1.0 / D) + 1e-06)
    normed = jnp.concatenate(
        [
            (
                stream_ref[c * rows : (c + 1) * rows, :].astype(F32)
                * factor
                * gain_ref[:, c * PART : (c + 1) * PART].astype(F32)
            ).astype(BF16)
            for c in range(PARTS)
        ],
        axis=0,
    )
    step = 384
    for s in range(0, place_ref.shape[0], step):
        out_ref[s : s + step, :] = jnp.dot(
            place_ref[s : s + step, :], normed, preferred_element_type=F32
        ).astype(BF16)


def expert_kernel(x_ref, w1_ref, w2_ref, out_ref, w1_buf, w2_buf, rows_ref, gated_ref, sem1, sem2):
    slots = rows_ref.shape[0]
    first = [
        pltpu.make_async_copy(
            w1_ref.at[pl.ds(c * PART, PART), :], w1_buf.at[pl.ds(c * PART, PART), :], sem1.at[c]
        )
        for c in range(PARTS)
    ]
    depth = EW // 3
    second = [
        pltpu.make_async_copy(
            w2_ref.at[pl.ds(j * depth, depth), :], w2_buf.at[pl.ds(j * depth, depth), :], sem2.at[j]
        )
        for j in range(3)
    ]
    for copy in first + second:
        copy.start()
    group = 32
    size = group * PARTS
    left = lax.broadcasted_iota(jnp.int32, (size, size), 0)
    right = lax.broadcasted_iota(jnp.int32, (size, size), 1)
    gather = ((left % group) * PARTS + left // group == right).astype(BF16)
    scatter = ((right % group) * PARTS + right // group == left).astype(BF16)
    for g in range(slots // group):
        moved = jnp.dot(
            gather, x_ref[g * size : (g + 1) * size, :], preferred_element_type=F32
        ).astype(BF16)
        for c in range(PARTS):
            rows_ref[g * group : (g + 1) * group, c * PART : (c + 1) * PART] = moved[
                c * group : (c + 1) * group, :
            ]
    for c in range(PARTS):
        first[c].wait()
        for n in range(0, 2 * EW, PART):
            part = jnp.dot(
                rows_ref[:, c * PART : (c + 1) * PART],
                w1_buf[c * PART : (c + 1) * PART, n : n + PART],
                preferred_element_type=F32,
            )
            if c == 0:
                gated_ref[:, n : n + PART] = part
            else:
                gated_ref[:, n : n + PART] += part
    gate = gated_ref[:, :EW]
    active = (gate / (1.0 + jnp.exp(-gate)) * gated_ref[:, EW:]).astype(BF16)
    for copy in second:
        copy.wait()
    for c in range(PARTS):
        rows_ref[:, c * PART : (c + 1) * PART] = jnp.dot(
            active, w2_buf[:, c * PART : (c + 1) * PART], preferred_element_type=F32
        ).astype(BF16)
    for g in range(slots // group):
        stacked = jnp.concatenate(
            [
                rows_ref[g * group : (g + 1) * group, c * PART : (c + 1) * PART]
                for c in range(PARTS)
            ],
            axis=0,
        )
        out_ref[g * size : (g + 1) * size, :] = jnp.dot(
            scatter, stacked, preferred_element_type=F32
        ).astype(BF16)


def combine_kernel(back_ref, mix_ref, stream_ref, out_ref):
    rows = out_ref.shape[0]
    mixture = jnp.dot(mix_ref[...], back_ref[...], preferred_element_type=F32)
    layer = (stream_ref[...].astype(F32) + mixture).astype(BF16)
    for c in range(PARTS):
        out_ref[:, c * PART : (c + 1) * PART] = layer[c * rows : (c + 1) * rows, :]


def call(kernel, outs, scratch, limit, flops, moved):
    return pl.pallas_call(
        kernel,
        out_shape=outs,
        scratch_shapes=scratch,
        compiler_params=pltpu.CompilerParams(vmem_limit_bytes=limit * MIB),
        cost_estimate=pl.CostEstimate(flops=flops, bytes_accessed=moved, transcendentals=0),
    )


def shards(
    tokens,
    queries,
    keys,
    values,
    output_weight,
    norm_gain,
    routing,
    gate_values,
    expand_weight,
    reduce_weight,
):
    length, pairs, local = queries.shape
    heads = local // HEAD_DIM
    context_size = lax.axis_size("ctx")
    expert_size = lax.axis_size("exp")
    experts = context_size * expert_size
    here = lax.axis_index("ctx")
    key_head = lax.axis_index("exp") * heads // (HEADS // KV_HEADS)
    rows = tokens.shape[0] * pairs
    slots = experts * CAP

    own = jnp.concatenate(
        [
            lax.dynamic_slice_in_dim(array, key_head * HEAD_DIM, HEAD_DIM, 2)
            for array in (keys, values)
        ],
        axis=2,
    ).reshape(length, pairs * 2 * HEAD_DIM)
    blocks = context_size // 2
    same = [[c for c in range(k, context_size, 2)] for k in range(2)]
    near = lax.all_to_all(
        jnp.broadcast_to(own[None], (blocks,) + own.shape),
        "ctx",
        0,
        0,
        axis_index_groups=same,
        tiled=True,
    )
    far = lax.ppermute(near, "ctx", [(c, c ^ 1) for c in range(context_size)])
    core = here % 2
    block = jnp.arange(blocks, dtype=jnp.int32) * 2
    positions = (
        jnp.concatenate([here[None].astype(jnp.int32), block + core, block + 1 - core]) * length
    )
    in_vmem = pl.BlockSpec(memory_space=pltpu.VMEM)
    projected = pl.pallas_call(
        functools.partial(
            attend_kernel, blocks=blocks, length=length, pairs=pairs, heads=heads
        ),
        out_shape=jax.ShapeDtypeStruct((expert_size, rows, D), BF16),
        in_specs=[pl.BlockSpec(memory_space=pltpu.SMEM)] + [in_vmem] * 4,
        out_specs=in_vmem,
        scratch_shapes=[pltpu.VMEM((2 * blocks, length, heads * length), F32)],
        compiler_params=pltpu.CompilerParams(vmem_limit_bytes=48 * MIB),
        cost_estimate=pl.CostEstimate(
            flops=2 * 10**9, bytes_accessed=9 * MIB, transcendentals=2 * 10**6
        ),
    )(positions, queries.reshape(length, pairs * local), near, far, output_weight)

    received = lax.all_to_all(projected, "exp", 0, 0, tiled=True)

    def pair_major(array):
        return jnp.swapaxes(array, 0, 1).reshape(rows, array.shape[2])

    place, mix = call(
        prepare_kernel,
        (
            jax.ShapeDtypeStruct((slots * PARTS, PARTS * rows), BF16),
            jax.ShapeDtypeStruct((PARTS * rows, slots * PARTS), BF16),
        ),
        [],
        32,
        10**9,
        3 * MIB,
    )(pair_major(routing), pair_major(gate_values))
    outgoing, stream = call(
        dispatch_kernel,
        (
            jax.ShapeDtypeStruct((slots * PARTS, PART), BF16),
            jax.ShapeDtypeStruct((PARTS * rows, PART), BF16),
        ),
        [],
        32,
        10**9,
        8 * MIB,
    )(received, pair_major(tokens), norm_gain[None], place)
    exchanged = (experts, CAP * PARTS, PART)
    arrived = lax.all_to_all(
        outgoing.reshape(exchanged), ("ctx", "exp"), 0, 0, tiled=True
    ).reshape(slots * PARTS, PART)
    anywhere = pl.BlockSpec(memory_space=pl.ANY)
    results = pl.pallas_call(
        expert_kernel,
        out_shape=jax.ShapeDtypeStruct((slots * PARTS, PART), BF16),
        in_specs=[in_vmem, anywhere, anywhere],
        out_specs=in_vmem,
        scratch_shapes=[
            pltpu.VMEM((D, 2 * EW), BF16),
            pltpu.VMEM((EW, D), BF16),
            pltpu.VMEM((slots, D), BF16),
            pltpu.VMEM((slots, 2 * EW), F32),
            pltpu.SemaphoreType.DMA((PARTS,)),
            pltpu.SemaphoreType.DMA((3,)),
        ],
        compiler_params=pltpu.CompilerParams(vmem_limit_bytes=48 * MIB),
        cost_estimate=pl.CostEstimate(
            flops=8 * 10**9, bytes_accessed=25 * MIB, transcendentals=3 * 10**5
        ),
    )(arrived, expand_weight[0], reduce_weight[0])
    returned = lax.all_to_all(
        results.reshape(exchanged), ("ctx", "exp"), 0, 0, tiled=True
    ).reshape(slots * PARTS, PART)
    layer = call(
        combine_kernel,
        jax.ShapeDtypeStruct((rows, D), BF16),
        [],
        32,
        10**9,
        5 * MIB,
    )(returned, mix, stream)
    return jnp.swapaxes(layer.reshape(pairs, tokens.shape[0], D), 0, 1)


def solution(mesh):
    in_specs = (
        P(("ctx", "exp"), None, None),
        P("ctx", None, "exp"),
        P("ctx", None, None),
        P("ctx", None, None),
        P("exp", None),
        P(),
        P(("ctx", "exp"), None, None),
        P(("ctx", "exp"), None, None),
        P(("ctx", "exp"), None, None),
        P(("ctx", "exp"), None, None),
    )
    out_specs = P(("ctx", "exp"), None, None)
    return jax.shard_map(shards, mesh=mesh, in_specs=in_specs, out_specs=out_specs, check_vma=False)
```

```python
import functools

import jax
import jax.numpy as jnp
from jax import lax
from jax.experimental import pallas as pl
from jax.experimental.pallas import tpu as pltpu
from jax.sharding import PartitionSpec as P

D = 4096
HEADS = 32
KV_HEADS = 2
HEAD_DIM = 128
EW = 768
TOP = 8
CAP = 3
PARTS = 8
PART = D // PARTS
LOG2E = 1.4426950408889634
F32 = jnp.float32
BF16 = jnp.bfloat16
MIB = 1 << 20


def contract(lhs, rhs, lhs_dim, rhs_dim):
    return lax.dot_general(
        lhs, rhs, (((lhs_dim,), (rhs_dim,)), ((), ())), preferred_element_type=F32
    )


def pack_kernel(info_ref, weight_ref, query_ref, out_ref, sem):
    depth = weight_ref.shape[0]
    width = out_ref.shape[1]
    extra = out_ref.shape[0] - depth
    cols = query_ref.shape[1]
    copies = [
        pltpu.make_async_copy(
            weight_ref.at[:, pl.ds(pl.multiple_of(info_ref[0], width), width)],
            out_ref.at[pl.ds(0, depth), :],
            sem.at[0],
        )
    ]
    for i in range(width // cols):
        copies.append(
            pltpu.make_async_copy(
                query_ref.at[pl.ds(i * extra, extra), :],
                out_ref.at[pl.ds(depth, extra), pl.ds(i * cols, cols)],
                sem.at[1 + i],
            )
        )
    for copy in copies:
        copy.start()
    for copy in copies:
        copy.wait()


def pieces(source, target, count, sem, first):
    size = source.shape[0] // count
    return [
        pltpu.make_async_copy(
            source.at[pl.ds(i * size, size), :],
            target.at[pl.ds(i * size, size), :],
            sem.at[first + i],
        )
        for i in range(count)
    ]


def attend_kernel(
    info_ref,
    q0_ref,
    own_ref,
    near_ref,
    far_ref,
    weight_ref,
    side_ref,
    expand_ref,
    reduce_ref,
    out_ref,
    low_out,
    high_out,
    reduce_out,
    score_ref,
    w0_ref,
    w1_ref,
    q1_ref,
    sem,
    *,
    pairs,
    heads,
):
    length = own_ref.shape[0]
    depth, half = w0_ref.shape
    extra = side_ref.shape[0] - depth
    cols = q1_ref.shape[1]
    copies = [
        pltpu.make_async_copy(
            side_ref.at[pl.ds(depth, extra), pl.ds(i * cols, cols)],
            q1_ref.at[pl.ds(i * extra, extra), :],
            sem.at[i],
        )
        for i in range(half // cols)
    ]
    moved = len(copies)
    copies.append(
        pltpu.make_async_copy(
            weight_ref.at[:, pl.ds(pl.multiple_of(info_ref[0], half), half)],
            w0_ref,
            sem.at[moved],
        )
    )
    copies.append(
        pltpu.make_async_copy(side_ref.at[pl.ds(0, depth), :], w1_ref, sem.at[moved + 1])
    )
    middle = low_out.shape[0]
    later_copies = pieces(expand_ref.at[pl.ds(0, middle), :], low_out, 4, sem, moved + 2)
    later_copies += pieces(expand_ref.at[pl.ds(middle, middle), :], high_out, 4, sem, moved + 6)
    later_copies += pieces(reduce_ref, reduce_out, 4, sem, moved + 10)
    for copy in copies + later_copies:
        copy.start()
    rows = heads * length
    scale = HEAD_DIM ** (-0.5) * LOG2E
    later = lax.broadcasted_iota(jnp.int32, (rows, length), 1) > (
        lax.broadcasted_iota(jnp.int32, (rows, length), 0) % length
    )
    span = 4 * length
    chunks = [
        (ref, start) for ref in (near_ref, far_ref) for start in range(0, ref.shape[0], span)
    ]
    groups = out_ref.shape[0]
    keep = length // groups
    stacked = []
    for q_ref in (q0_ref, q1_ref):
        if q_ref is q1_ref:
            for copy in copies[:moved]:
                copy.wait()
        attended = []
        for p in range(pairs):
            keys = slice(p * 2 * HEAD_DIM, (p * 2 + 1) * HEAD_DIM)
            values = slice((p * 2 + 1) * HEAD_DIM, (p * 2 + 2) * HEAD_DIM)
            first = p * heads * HEAD_DIM
            query = jnp.concatenate(
                [
                    q_ref[:, first + h * HEAD_DIM : first + (h + 1) * HEAD_DIM]
                    for h in range(heads)
                ],
                axis=0,
            )
            score = jnp.where(later, -1e30, contract(query, own_ref[:, keys], 1, 1))
            score_ref[:, :length] = score
            peak = score
            for i, (ref, start) in enumerate(chunks):
                score = contract(query, ref[start : start + span, keys], 1, 1)
                for j in range(0, span, length):
                    earlier = info_ref[1 + (i * span + j) // length] > 0
                    part = jnp.where(earlier, score[:, j : j + length], -1e30)
                    at = length + i * span + j
                    score_ref[:, at : at + length] = part
                    peak = jnp.maximum(peak, part)
            peak = jnp.max(peak, axis=1, keepdims=True)
            weight = jnp.exp2((score_ref[:, :length] - peak) * scale)
            mass = weight
            acc = jnp.dot(weight.astype(BF16), own_ref[:, values], preferred_element_type=F32)
            for i, (ref, start) in enumerate(chunks):
                at = length + i * span
                weight = jnp.exp2((score_ref[:, at : at + span] - peak) * scale)
                for j in range(0, span, length):
                    mass = mass + weight[:, j : j + length]
                acc = acc + jnp.dot(
                    weight.astype(BF16),
                    ref[start : start + span, values],
                    preferred_element_type=F32,
                )
            acc = (acc / jnp.sum(mass, axis=1, keepdims=True)).astype(BF16)
            attended.append(
                jnp.concatenate(
                    [acc[h * length : (h + 1) * length] for h in range(heads)], axis=1
                )
            )
        stacked.append(jnp.concatenate(attended, axis=0))
    for copy in copies[moved:]:
        copy.wait()
    step = half // 4
    for n in range(0, half, step):
        part = jnp.dot(stacked[0], w0_ref[:, n : n + step], preferred_element_type=F32)
        part = part + jnp.dot(stacked[1], w1_ref[:, n : n + step], preferred_element_type=F32)
        part = part.astype(BF16)
        for p in range(pairs):
            out_ref[:, p * keep : (p + 1) * keep, n : n + step] = part[
                p * length : (p + 1) * length
            ].reshape(groups, keep, step)
    for copy in later_copies:
        copy.wait()


def prepare_kernel(routing_ref, gate_ref, place_ref, mix_ref):
    rows = routing_ref.shape[0]
    experts = place_ref.shape[0] // (CAP * PARTS)
    slots = place_ref.shape[0]
    width = PARTS * rows
    expert_iota = lax.broadcasted_iota(jnp.int32, (rows, experts), 1)
    named = jnp.zeros((rows, experts), F32)
    gates = jnp.zeros((rows, experts), F32)
    for k in range(TOP):
        hit = routing_ref[:, k : k + 1] == expert_iota
        named = jnp.where(hit, 1.0, named)
        gates = jnp.where(hit, gate_ref[:, k : k + 1], gates)
    lower = (
        lax.broadcasted_iota(jnp.int32, (rows, rows), 0)
        >= lax.broadcasted_iota(jnp.int32, (rows, rows), 1)
    ).astype(BF16)
    rank = named * jnp.dot(lower, named.astype(BF16), preferred_element_type=F32)
    spread = (
        lax.broadcasted_iota(jnp.int32, (rows, width), 0)
        == lax.broadcasted_iota(jnp.int32, (rows, width), 1) % rows
    ).astype(BF16)
    wide = contract(rank.astype(BF16), spread, 0, 0).astype(BF16)
    chunk = 768
    for s in range(0, slots, chunk):
        slot = s + lax.broadcasted_iota(jnp.int32, (chunk, experts), 0)
        owner = (
            slot // (CAP * PARTS) == lax.broadcasted_iota(jnp.int32, (chunk, experts), 1)
        ).astype(BF16)
        ranks = jnp.dot(owner, wide, preferred_element_type=F32)
        row = s + lax.broadcasted_iota(jnp.int32, (chunk, width), 0)
        col = lax.broadcasted_iota(jnp.int32, (chunk, width), 1)
        hit = (ranks == (row // PARTS % CAP + 1).astype(F32)) & (row % PARTS == col // rows)
        place_ref[s : s + chunk, :] = hit.astype(BF16)
        slot = s + lax.broadcasted_iota(jnp.int32, (experts, chunk), 1)
        owner = (
            slot // (CAP * PARTS) == lax.broadcasted_iota(jnp.int32, (experts, chunk), 0)
        ).astype(BF16)
        ranks = jnp.dot(rank.astype(BF16), owner, preferred_element_type=F32)
        value = jnp.dot(gates.astype(BF16), owner, preferred_element_type=F32)
        col = s + lax.broadcasted_iota(jnp.int32, (rows, chunk), 1)
        value = jnp.where(ranks == (col // PARTS % CAP + 1).astype(F32), value, 0.0)
        for c in range(PARTS):
            mix_ref[c * rows : (c + 1) * rows, s : s + chunk] = jnp.where(
                col % PARTS == c, value, 0.0
            ).astype(BF16)


def dispatch_kernel(
    part_ref, token_ref, gain_ref, place_ref, out_ref, stream_ref
):
    sources = part_ref.shape[0]
    rows = token_ref.shape[0]
    half = PARTS // 2
    square = jnp.zeros((rows, 1), F32)
    for c in range(PARTS):
        at = slice(c % half * PART, (c % half + 1) * PART)
        total = token_ref[:, c * PART : (c + 1) * PART].astype(F32)
        total = total + sum(
            part_ref[s, :, at].astype(F32) for s in range(c // half, sources, 2)
        )
        stream = total.astype(BF16)
        stream_ref[c * rows : (c + 1) * rows, :] = stream
        wide = stream.astype(F32)
        square = square + jnp.sum(wide * wide, axis=1, keepdims=True)
    factor = lax.rsqrt(square * (1.0 / D) + 1e-06)
    normed = jnp.concatenate(
        [
            (
                stream_ref[c * rows : (c + 1) * rows, :].astype(F32)
                * factor
                * gain_ref[:, c * PART : (c + 1) * PART].astype(F32)
            ).astype(BF16)
            for c in range(PARTS)
        ],
        axis=0,
    )
    step = 384
    for s in range(0, place_ref.shape[0], step):
        out_ref[s : s + step, :] = jnp.dot(
            place_ref[s : s + step, :], normed, preferred_element_type=F32
        ).astype(BF16)


def expert_kernel(x_ref, low_ref, high_ref, w2_ref, out_ref, rows_ref, gated_ref):
    slots = rows_ref.shape[0]
    group = 32
    size = group * PARTS
    left = lax.broadcasted_iota(jnp.int32, (size, size), 0)
    right = lax.broadcasted_iota(jnp.int32, (size, size), 1)
    gather = ((left % group) * PARTS + left // group == right).astype(BF16)
    scatter = ((right % group) * PARTS + right // group == left).astype(BF16)
    for g in range(slots // group):
        moved = jnp.dot(
            gather, x_ref[g * size : (g + 1) * size, :], preferred_element_type=F32
        ).astype(BF16)
        for c in range(PARTS):
            rows_ref[g * group : (g + 1) * group, c * PART : (c + 1) * PART] = moved[
                c * group : (c + 1) * group, :
            ]
    for c in range(PARTS):
        half_ref = low_ref if c < PARTS // 2 else high_ref
        at = c * PART % half_ref.shape[0]
        for n in range(0, 2 * EW, PART):
            part = jnp.dot(
                rows_ref[:, c * PART : (c + 1) * PART],
                half_ref[at : at + PART, n : n + PART],
                preferred_element_type=F32,
            )
            if c == 0:
                gated_ref[:, n : n + PART] = part
            else:
                gated_ref[:, n : n + PART] += part
    gate = gated_ref[:, :EW]
    active = (gate / (1.0 + jnp.exp(-gate)) * gated_ref[:, EW:]).astype(BF16)
    for c in range(PARTS):
        rows_ref[:, c * PART : (c + 1) * PART] = jnp.dot(
            active, w2_ref[:, c * PART : (c + 1) * PART], preferred_element_type=F32
        ).astype(BF16)
    for g in range(slots // group):
        stacked = jnp.concatenate(
            [
                rows_ref[g * group : (g + 1) * group, c * PART : (c + 1) * PART]
                for c in range(PARTS)
            ],
            axis=0,
        )
        out_ref[g * size : (g + 1) * size, :] = jnp.dot(
            scatter, stacked, preferred_element_type=F32
        ).astype(BF16)


def combine_kernel(back_ref, mix_ref, stream_ref, out_ref):
    rows = out_ref.shape[0]
    mixture = jnp.dot(mix_ref[...], back_ref[...], preferred_element_type=F32)
    layer = (stream_ref[...].astype(F32) + mixture).astype(BF16)
    for c in range(PARTS):
        out_ref[:, c * PART : (c + 1) * PART] = layer[c * rows : (c + 1) * rows, :]


def call(kernel, outs, scratch, limit, flops, moved):
    return pl.pallas_call(
        kernel,
        out_shape=outs,
        scratch_shapes=scratch,
        compiler_params=pltpu.CompilerParams(vmem_limit_bytes=limit * MIB),
        cost_estimate=pl.CostEstimate(flops=flops, bytes_accessed=moved, transcendentals=0),
    )


def shards(
    tokens,
    queries,
    keys,
    values,
    output_weight,
    norm_gain,
    routing,
    gate_values,
    expand_weight,
    reduce_weight,
):
    length, pairs, local = queries.shape
    heads = local // HEAD_DIM
    context_size = lax.axis_size("ctx")
    expert_size = lax.axis_size("exp")
    experts = context_size * expert_size
    here = lax.axis_index("ctx")
    key_head = lax.axis_index("exp") * heads // (HEADS // KV_HEADS)
    rows = tokens.shape[0] * pairs
    slots = experts * CAP

    own = jnp.concatenate(
        [
            lax.dynamic_slice_in_dim(array, key_head * HEAD_DIM, HEAD_DIM, 2)
            for array in (keys, values)
        ],
        axis=2,
    ).reshape(length, pairs * 2 * HEAD_DIM)
    blocks = context_size // 2
    core = here % 2
    side = lax.axis_index("exp") % 2
    swap_core = [(c, c ^ 1) for c in range(context_size)]
    swap_side = [
        (c * expert_size + e, c * expert_size + (e ^ (1 + 2 * (c % 2))))
        for c in range(context_size)
        for e in range(expert_size)
    ]
    hbm_weight = pltpu.with_memory_space_constraint(output_weight, pltpu.HBM)
    half = D // 2
    query = queries.reshape(length, pairs * local)
    in_vmem = pl.BlockSpec(memory_space=pltpu.VMEM)
    anywhere = pl.BlockSpec(memory_space=pl.ANY)
    in_smem = pl.BlockSpec(memory_space=pltpu.SMEM)
    sent = pl.pallas_call(
        pack_kernel,
        out_shape=pltpu.VMEM((local + length * pairs * local // half, half), BF16),
        in_specs=[in_smem, pl.BlockSpec(memory_space=pltpu.HBM), anywhere],
        out_specs=in_vmem,
        scratch_shapes=[pltpu.SemaphoreType.DMA((1 + half // (pairs * local),))],
        compiler_params=pltpu.CompilerParams(vmem_limit_bytes=4 * MIB),
        cost_estimate=pl.CostEstimate(flops=0, bytes_accessed=5 * MIB, transcendentals=0),
    )(((1 - side) * half).astype(jnp.int32)[None], hbm_weight, query)
    from_side = lax.ppermute(sent, ("ctx", "exp"), swap_side)
    same = [[c for c in range(k, context_size, 2)] for k in range(2)]
    near = lax.all_to_all(
        jnp.broadcast_to(own[None], (blocks,) + own.shape),
        "ctx",
        0,
        0,
        axis_index_groups=same,
        tiled=True,
    )
    far = lax.ppermute(near, "ctx", swap_core)
    block = jnp.arange(blocks, dtype=jnp.int32) * 2
    order = jnp.concatenate([block + core, block + 1 - core])
    info = jnp.concatenate(
        [(side * half).astype(jnp.int32)[None], (order < here).astype(jnp.int32)]
    )
    def pair_major(array):
        return jnp.swapaxes(array, 0, 1).reshape(rows, array.shape[2])

    place, mix = call(
        prepare_kernel,
        (
            pltpu.VMEM((slots * PARTS, PARTS * rows), BF16),
            jax.ShapeDtypeStruct((PARTS * rows, slots * PARTS), BF16),
        ),
        [],
        8,
        10**9,
        3 * MIB,
    )(pair_major(routing), pair_major(gate_values))
    token_rows, gain = pair_major(tokens), norm_gain[None]
    info, place, mix, token_rows, gain = lax.optimization_barrier(
        (info, place, mix, token_rows, gain)
    )
    in_hbm = pl.BlockSpec(memory_space=pltpu.HBM)
    projected, low, high, reduce = pl.pallas_call(
        functools.partial(attend_kernel, pairs=pairs, heads=heads),
        out_shape=(
            jax.ShapeDtypeStruct((expert_size, rows, half), BF16),
            pltpu.VMEM((D // 2, 2 * EW), BF16),
            pltpu.VMEM((D // 2, 2 * EW), BF16),
            pltpu.VMEM((EW, D), BF16),
        ),
        in_specs=[in_smem] + [in_vmem] * 4 + [in_hbm, anywhere, in_hbm, in_hbm],
        out_specs=(in_vmem,) * 4,
        scratch_shapes=[
            pltpu.VMEM((heads * length, (context_size + 1) * length), F32),
            pltpu.VMEM((local, half), BF16),
            pltpu.VMEM((local, half), BF16),
            pltpu.VMEM((length, pairs * local), BF16),
            pltpu.SemaphoreType.DMA((16,)),
        ],
        compiler_params=pltpu.CompilerParams(vmem_limit_bytes=16 * MIB),
        cost_estimate=pl.CostEstimate(
            flops=3 * 10**9, bytes_accessed=9 * MIB, transcendentals=4 * 10**6
        ),
    )(
        info,
        query,
        own,
        near.reshape(blocks * length, -1),
        far.reshape(blocks * length, -1),
        hbm_weight,
        from_side,
        pltpu.with_memory_space_constraint(expand_weight[0], pltpu.HBM),
        pltpu.with_memory_space_constraint(reduce_weight[0], pltpu.HBM),
    )

    received = lax.all_to_all(projected, "exp", 0, 0, tiled=True)

    outgoing, stream = pl.pallas_call(
        dispatch_kernel,
        out_shape=(
            jax.ShapeDtypeStruct((slots * PARTS, PART), BF16),
            jax.ShapeDtypeStruct((PARTS * rows, PART), BF16),
        ),
        in_specs=[in_vmem] * 4,
        out_specs=(in_vmem, in_vmem),
        compiler_params=pltpu.CompilerParams(vmem_limit_bytes=8 * MIB),
        cost_estimate=pl.CostEstimate(
            flops=10**9, bytes_accessed=7 * MIB, transcendentals=0
        ),
    )(received, token_rows, gain, pltpu.with_memory_space_constraint(place, pltpu.VMEM))
    exchanged = (experts, CAP * PARTS, PART)
    arrived = lax.all_to_all(
        outgoing.reshape(exchanged), ("ctx", "exp"), 0, 0, tiled=True
    ).reshape(slots * PARTS, PART)
    results = pl.pallas_call(
        expert_kernel,
        out_shape=jax.ShapeDtypeStruct((slots * PARTS, PART), BF16),
        in_specs=[in_vmem] * 4,
        out_specs=in_vmem,
        scratch_shapes=[pltpu.VMEM((slots, D), BF16), pltpu.VMEM((slots, 2 * EW), F32)],
        compiler_params=pltpu.CompilerParams(vmem_limit_bytes=10 * MIB),
        cost_estimate=pl.CostEstimate(
            flops=8 * 10**9, bytes_accessed=6 * MIB, transcendentals=3 * 10**5
        ),
    )(
        arrived,
        pltpu.with_memory_space_constraint(low, pltpu.VMEM),
        pltpu.with_memory_space_constraint(high, pltpu.VMEM),
        pltpu.with_memory_space_constraint(reduce, pltpu.VMEM),
    )
    returned = lax.all_to_all(
        results.reshape(exchanged), ("ctx", "exp"), 0, 0, tiled=True
    ).reshape(slots * PARTS, PART)
    layer = call(
        combine_kernel,
        jax.ShapeDtypeStruct((rows, D), BF16),
        [],
        8,
        10**9,
        5 * MIB,
    )(returned, mix, stream)
    return jnp.swapaxes(layer.reshape(pairs, tokens.shape[0], D), 0, 1)


def solution(mesh):
    in_specs = (
        P(("ctx", "exp"), None, None),
        P("ctx", None, "exp"),
        P("ctx", None, None),
        P("ctx", None, None),
        P("exp", None),
        P(),
        P(("ctx", "exp"), None, None),
        P(("ctx", "exp"), None, None),
        P(("ctx", "exp"), None, None),
        P(("ctx", "exp"), None, None),
    )
    out_specs = P(("ctx", "exp"), None, None)
    return jax.shard_map(shards, mesh=mesh, in_specs=in_specs, out_specs=out_specs, check_vma=False)
```

```python
import functools

import jax
import jax.numpy as jnp
from jax import lax
from jax.experimental import pallas as pl
from jax.experimental.pallas import tpu as pltpu
from jax.sharding import PartitionSpec as P

D = 4096
HEADS = 32
KV_HEADS = 2
HEAD_DIM = 128
EW = 768
TOP = 8
CAP = 3
PARTS = 8
PART = D // PARTS
LOG2E = 1.4426950408889634
F32 = jnp.float32
BF16 = jnp.bfloat16
MIB = 1 << 20


def contract(lhs, rhs, lhs_dim, rhs_dim):
    return lax.dot_general(
        lhs, rhs, (((lhs_dim,), (rhs_dim,)), ((), ())), preferred_element_type=F32
    )


def pieces(source, target, count, sem, first):
    size = source.shape[0] // count
    return [
        pltpu.make_async_copy(
            source.at[pl.ds(i * size, size), :],
            target.at[pl.ds(i * size, size), :],
            sem.at[first + i],
        )
        for i in range(count)
    ]


def pack_kernel(info_ref, weight_ref, query_ref, out_ref, sem):
    depth = weight_ref.shape[0]
    width = out_ref.shape[1]
    extra = out_ref.shape[0] - depth
    cols = query_ref.shape[1]
    columns = weight_ref.at[:, pl.ds(pl.multiple_of(info_ref[0], width), width)]
    copies = pieces(columns, out_ref.at[pl.ds(0, depth), :], 8, sem, 0)
    for i in range(width // cols):
        copies.append(
            pltpu.make_async_copy(
                query_ref.at[pl.ds(i * extra, extra), :],
                out_ref.at[pl.ds(depth, extra), pl.ds(i * cols, cols)],
                sem.at[8 + i],
            )
        )
    for copy in copies:
        copy.start()
    for copy in copies:
        copy.wait()


def attend_kernel(
    info_ref,
    q0_ref,
    own_ref,
    near_ref,
    far_ref,
    weight_ref,
    side_ref,
    out_ref,
    score_ref,
    bias_ref,
    w0_ref,
    w1_ref,
    q1_ref,
    sem,
    *,
    pairs,
    heads,
):
    length = own_ref.shape[0]
    depth, half = w0_ref.shape
    extra = side_ref.shape[0] - depth
    cols = q1_ref.shape[1]
    copies = [
        pltpu.make_async_copy(
            side_ref.at[pl.ds(depth, extra), pl.ds(i * cols, cols)],
            q1_ref.at[pl.ds(i * extra, extra), :],
            sem.at[i],
        )
        for i in range(half // cols)
    ]
    moved = len(copies)
    copies.append(
        pltpu.make_async_copy(
            weight_ref.at[:, pl.ds(pl.multiple_of(info_ref[0], half), half)],
            w0_ref,
            sem.at[moved],
        )
    )
    copies.append(
        pltpu.make_async_copy(side_ref.at[pl.ds(0, depth), :], w1_ref, sem.at[moved + 1])
    )
    for copy in copies:
        copy.start()
    rows = heads * length
    scale = HEAD_DIM ** (-0.5) * LOG2E
    later = lax.broadcasted_iota(jnp.int32, (rows, length), 1) > (
        lax.broadcasted_iota(jnp.int32, (rows, length), 0) % length
    )
    span = 8 * length
    chunks = [
        (ref, start) for ref in (near_ref, far_ref) for start in range(0, ref.shape[0], span)
    ]
    one = (lax.broadcasted_iota(jnp.int32, (rows, HEAD_DIM), 1) == 0).astype(BF16)
    for i in range(len(chunks)):
        for j in range(span // length):
            hidden = jnp.where(info_ref[1 + i * (span // length) + j] > 0, 0.0, -1e30)
            bias_ref[i, j * length : (j + 1) * length, :] = jnp.full(
                (length, HEAD_DIM), hidden, F32
            ).astype(BF16)
    groups = out_ref.shape[0]
    keep = length // groups
    stacked = []
    for q_ref in (q0_ref, q1_ref):
        if q_ref is q1_ref:
            for copy in copies[:moved]:
                copy.wait()
        attended = []
        for p in range(pairs):
            keys = slice(p * 2 * HEAD_DIM, (p * 2 + 1) * HEAD_DIM)
            values = slice((p * 2 + 1) * HEAD_DIM, (p * 2 + 2) * HEAD_DIM)
            first = p * heads * HEAD_DIM
            query = jnp.concatenate(
                [
                    q_ref[:, first + h * HEAD_DIM : first + (h + 1) * HEAD_DIM]
                    for h in range(heads)
                ],
                axis=0,
            )
            score = jnp.where(later, -1e30, contract(query, own_ref[:, keys], 1, 1))
            score_ref[:, :length] = score
            peak = score
            marked = jnp.concatenate([query, one], axis=1)
            for i, (ref, start) in enumerate(chunks):
                key = jnp.concatenate([ref[start : start + span, keys], bias_ref[i]], axis=1)
                score = contract(marked, key, 1, 1)
                at = length + i * span
                score_ref[:, at : at + span] = score
                for j in range(0, span, length):
                    peak = jnp.maximum(peak, score[:, j : j + length])
            peak = jnp.max(peak, axis=1, keepdims=True)
            weight = jnp.exp2((score_ref[:, :length] - peak) * scale)
            mass = weight
            acc = jnp.dot(weight.astype(BF16), own_ref[:, values], preferred_element_type=F32)
            for i, (ref, start) in enumerate(chunks):
                at = length + i * span
                weight = jnp.exp2((score_ref[:, at : at + span] - peak) * scale)
                for j in range(0, span, length):
                    mass = mass + weight[:, j : j + length]
                acc = acc + jnp.dot(
                    weight.astype(BF16),
                    ref[start : start + span, values],
                    preferred_element_type=F32,
                )
            acc = (acc / jnp.sum(mass, axis=1, keepdims=True)).astype(BF16)
            attended.append(
                jnp.concatenate(
                    [acc[h * length : (h + 1) * length] for h in range(heads)], axis=1
                )
            )
        stacked.append(jnp.concatenate(attended, axis=0))
    for copy in copies[moved:]:
        copy.wait()
    step = half // 4
    for n in range(0, half, step):
        part = jnp.dot(stacked[0], w0_ref[:, n : n + step], preferred_element_type=F32)
        part = part + jnp.dot(stacked[1], w1_ref[:, n : n + step], preferred_element_type=F32)
        part = part.astype(BF16)
        for p in range(pairs):
            out_ref[:, p * keep : (p + 1) * keep, n : n + step] = part[
                p * length : (p + 1) * length
            ].reshape(groups, keep, step)


def prepare_kernel(routing_ref, gate_ref, place_ref, mix_ref):
    rows = routing_ref.shape[0]
    experts = place_ref.shape[0] // (CAP * PARTS)
    slots = place_ref.shape[0]
    width = PARTS * rows
    expert_iota = lax.broadcasted_iota(jnp.int32, (rows, experts), 1)
    named = jnp.zeros((rows, experts), F32)
    gates = jnp.zeros((rows, experts), F32)
    for k in range(TOP):
        hit = routing_ref[:, k : k + 1] == expert_iota
        named = jnp.where(hit, 1.0, named)
        gates = jnp.where(hit, gate_ref[:, k : k + 1], gates)
    lower = (
        lax.broadcasted_iota(jnp.int32, (rows, rows), 0)
        >= lax.broadcasted_iota(jnp.int32, (rows, rows), 1)
    ).astype(BF16)
    rank = named * jnp.dot(lower, named.astype(BF16), preferred_element_type=F32)
    spread = (
        lax.broadcasted_iota(jnp.int32, (rows, width), 0)
        == lax.broadcasted_iota(jnp.int32, (rows, width), 1) % rows
    ).astype(BF16)
    wide = contract(rank.astype(BF16), spread, 0, 0).astype(BF16)
    chunk = 768
    for s in range(0, slots, chunk):
        slot = s + lax.broadcasted_iota(jnp.int32, (chunk, experts), 0)
        owner = (
            slot // (CAP * PARTS) == lax.broadcasted_iota(jnp.int32, (chunk, experts), 1)
        ).astype(BF16)
        ranks = jnp.dot(owner, wide, preferred_element_type=F32)
        row = s + lax.broadcasted_iota(jnp.int32, (chunk, width), 0)
        col = lax.broadcasted_iota(jnp.int32, (chunk, width), 1)
        hit = (ranks == (row // PARTS % CAP + 1).astype(F32)) & (row % PARTS == col // rows)
        place_ref[s : s + chunk, :] = hit.astype(BF16)
        slot = s + lax.broadcasted_iota(jnp.int32, (experts, chunk), 1)
        owner = (
            slot // (CAP * PARTS) == lax.broadcasted_iota(jnp.int32, (experts, chunk), 0)
        ).astype(BF16)
        ranks = jnp.dot(rank.astype(BF16), owner, preferred_element_type=F32)
        value = jnp.dot(gates.astype(BF16), owner, preferred_element_type=F32)
        col = s + lax.broadcasted_iota(jnp.int32, (rows, chunk), 1)
        value = jnp.where(ranks == (col // PARTS % CAP + 1).astype(F32), value, 0.0)
        for c in range(PARTS):
            mix_ref[c * rows : (c + 1) * rows, s : s + chunk] = jnp.where(
                col % PARTS == c, value, 0.0
            ).astype(BF16)


def dispatch_kernel(
    part_ref, token_ref, gain_ref, place_ref, out_ref, stream_ref
):
    sources = part_ref.shape[0]
    rows = token_ref.shape[0]
    half = PARTS // 2
    square = jnp.zeros((rows, 1), F32)
    for c in range(PARTS):
        at = slice(c % half * PART, (c % half + 1) * PART)
        total = token_ref[:, c * PART : (c + 1) * PART].astype(F32)
        total = total + sum(
            part_ref[s, :, at].astype(F32) for s in range(c // half, sources, 2)
        )
        stream = total.astype(BF16)
        stream_ref[c * rows : (c + 1) * rows, :] = stream
        wide = stream.astype(F32)
        square = square + jnp.sum(wide * wide, axis=1, keepdims=True)
    factor = lax.rsqrt(square * (1.0 / D) + 1e-06)
    normed = jnp.concatenate(
        [
            (
                stream_ref[c * rows : (c + 1) * rows, :].astype(F32)
                * factor
                * gain_ref[:, c * PART : (c + 1) * PART].astype(F32)
            ).astype(BF16)
            for c in range(PARTS)
        ],
        axis=0,
    )
    step = 384
    for s in range(0, place_ref.shape[0], step):
        out_ref[s : s + step, :] = jnp.dot(
            place_ref[s : s + step, :], normed, preferred_element_type=F32
        ).astype(BF16)


def expert_kernel(x_ref, w1_ref, w2_ref, out_ref, rows_ref, gated_ref):
    slots = rows_ref.shape[0]
    group = 32
    size = group * PARTS
    left = lax.broadcasted_iota(jnp.int32, (size, size), 0)
    right = lax.broadcasted_iota(jnp.int32, (size, size), 1)
    gather = ((left % group) * PARTS + left // group == right).astype(BF16)
    scatter = ((right % group) * PARTS + right // group == left).astype(BF16)
    for g in range(slots // group):
        moved = jnp.dot(
            gather, x_ref[g * size : (g + 1) * size, :], preferred_element_type=F32
        ).astype(BF16)
        for c in range(PARTS):
            rows_ref[g * group : (g + 1) * group, c * PART : (c + 1) * PART] = moved[
                c * group : (c + 1) * group, :
            ]
    for c in range(PARTS):
        for n in range(0, 2 * EW, PART):
            part = jnp.dot(
                rows_ref[:, c * PART : (c + 1) * PART],
                w1_ref[c * PART : (c + 1) * PART, n : n + PART],
                preferred_element_type=F32,
            )
            if c == 0:
                gated_ref[:, n : n + PART] = part
            else:
                gated_ref[:, n : n + PART] += part
    gate = gated_ref[:, :EW]
    active = (gate / (1.0 + jnp.exp(-gate)) * gated_ref[:, EW:]).astype(BF16)
    for c in range(PARTS):
        rows_ref[:, c * PART : (c + 1) * PART] = jnp.dot(
            active, w2_ref[:, c * PART : (c + 1) * PART], preferred_element_type=F32
        ).astype(BF16)
    for g in range(slots // group):
        stacked = jnp.concatenate(
            [
                rows_ref[g * group : (g + 1) * group, c * PART : (c + 1) * PART]
                for c in range(PARTS)
            ],
            axis=0,
        )
        out_ref[g * size : (g + 1) * size, :] = jnp.dot(
            scatter, stacked, preferred_element_type=F32
        ).astype(BF16)


def combine_kernel(back_ref, mix_ref, stream_ref, out_ref):
    rows = out_ref.shape[0]
    mixture = jnp.dot(mix_ref[...], back_ref[...], preferred_element_type=F32)
    layer = (stream_ref[...].astype(F32) + mixture).astype(BF16)
    for c in range(PARTS):
        out_ref[:, c * PART : (c + 1) * PART] = layer[c * rows : (c + 1) * rows, :]


def call(kernel, outs, scratch, limit, flops, moved):
    return pl.pallas_call(
        kernel,
        out_shape=outs,
        scratch_shapes=scratch,
        compiler_params=pltpu.CompilerParams(vmem_limit_bytes=limit * MIB),
        cost_estimate=pl.CostEstimate(flops=flops, bytes_accessed=moved, transcendentals=0),
    )


def shards(
    tokens,
    queries,
    keys,
    values,
    output_weight,
    norm_gain,
    routing,
    gate_values,
    expand_weight,
    reduce_weight,
):
    length, pairs, local = queries.shape
    heads = local // HEAD_DIM
    context_size = lax.axis_size("ctx")
    expert_size = lax.axis_size("exp")
    experts = context_size * expert_size
    here = lax.axis_index("ctx")
    key_head = lax.axis_index("exp") * heads // (HEADS // KV_HEADS)
    rows = tokens.shape[0] * pairs
    slots = experts * CAP

    own = jnp.concatenate(
        [
            lax.dynamic_slice_in_dim(array, key_head * HEAD_DIM, HEAD_DIM, 2)
            for array in (keys, values)
        ],
        axis=2,
    ).reshape(length, pairs * 2 * HEAD_DIM)
    blocks = context_size // 2
    core = here % 2
    side = lax.axis_index("exp") % 2
    swap_core = [(c, c ^ 1) for c in range(context_size)]
    swap_side = [
        (c * expert_size + e, c * expert_size + (e ^ (1 + 2 * (c % 2))))
        for c in range(context_size)
        for e in range(expert_size)
    ]
    hbm_weight = pltpu.with_memory_space_constraint(output_weight, pltpu.HBM)
    half = D // 2
    query = queries.reshape(length, pairs * local)
    in_vmem = pl.BlockSpec(memory_space=pltpu.VMEM)
    anywhere = pl.BlockSpec(memory_space=pl.ANY)
    in_smem = pl.BlockSpec(memory_space=pltpu.SMEM)
    sent = pl.pallas_call(
        pack_kernel,
        out_shape=pltpu.VMEM((local + length * pairs * local // half, half), BF16),
        in_specs=[in_smem, pl.BlockSpec(memory_space=pltpu.HBM), anywhere],
        out_specs=in_vmem,
        scratch_shapes=[pltpu.SemaphoreType.DMA((8 + half // (pairs * local),))],
        compiler_params=pltpu.CompilerParams(vmem_limit_bytes=4 * MIB),
        cost_estimate=pl.CostEstimate(flops=0, bytes_accessed=5 * MIB, transcendentals=0),
    )(((1 - side) * half).astype(jnp.int32)[None], hbm_weight, query)
    from_side = lax.ppermute(sent, ("ctx", "exp"), swap_side)
    same = [[c for c in range(k, context_size, 2)] for k in range(2)]
    near = lax.all_to_all(
        jnp.broadcast_to(own[None], (blocks,) + own.shape),
        "ctx",
        0,
        0,
        axis_index_groups=same,
        tiled=True,
    )
    far = lax.ppermute(near, "ctx", swap_core)
    block = jnp.arange(blocks, dtype=jnp.int32) * 2
    order = jnp.concatenate([block + core, block + 1 - core])
    info = jnp.concatenate(
        [(side * half).astype(jnp.int32)[None], (order < here).astype(jnp.int32)]
    )
    def pair_major(array):
        return jnp.swapaxes(array, 0, 1).reshape(rows, array.shape[2])

    place, mix = call(
        prepare_kernel,
        (
            pltpu.VMEM((slots * PARTS, PARTS * rows), BF16),
            jax.ShapeDtypeStruct((PARTS * rows, slots * PARTS), BF16),
        ),
        [],
        8,
        10**9,
        3 * MIB,
    )(pair_major(routing), pair_major(gate_values))
    token_rows, gain = pair_major(tokens), norm_gain[None]
    info, place, mix, token_rows, gain = lax.optimization_barrier(
        (info, place, mix, token_rows, gain)
    )
    in_hbm = pl.BlockSpec(memory_space=pltpu.HBM)
    projected = pl.pallas_call(
        functools.partial(attend_kernel, pairs=pairs, heads=heads),
        out_shape=jax.ShapeDtypeStruct((expert_size, rows, half), BF16),
        in_specs=[in_smem] + [in_vmem] * 4 + [in_hbm] * 2,
        out_specs=in_vmem,
        scratch_shapes=[
            pltpu.VMEM((heads * length, (context_size + 1) * length), F32),
            pltpu.VMEM((2, blocks * length, HEAD_DIM), BF16),
            pltpu.VMEM((local, half), BF16),
            pltpu.VMEM((local, half), BF16),
            pltpu.VMEM((length, pairs * local), BF16),
            pltpu.SemaphoreType.DMA((16,)),
        ],
        compiler_params=pltpu.CompilerParams(vmem_limit_bytes=22 * MIB),
        cost_estimate=pl.CostEstimate(
            flops=3 * 10**9, bytes_accessed=9 * MIB, transcendentals=4 * 10**6
        ),
    )(
        info,
        query,
        own,
        pltpu.with_memory_space_constraint(near.reshape(blocks * length, -1), pltpu.VMEM),
        pltpu.with_memory_space_constraint(far.reshape(blocks * length, -1), pltpu.VMEM),
        hbm_weight,
        pltpu.with_memory_space_constraint(from_side, pltpu.HBM),
    )

    projected, expand, reduce = lax.optimization_barrier(
        (projected, expand_weight[0], reduce_weight[0])
    )
    received = lax.all_to_all(projected, "exp", 0, 0, tiled=True)

    outgoing, stream = pl.pallas_call(
        dispatch_kernel,
        out_shape=(
            jax.ShapeDtypeStruct((slots * PARTS, PART), BF16),
            jax.ShapeDtypeStruct((PARTS * rows, PART), BF16),
        ),
        in_specs=[in_vmem] * 4,
        out_specs=(in_vmem, in_vmem),
        compiler_params=pltpu.CompilerParams(vmem_limit_bytes=8 * MIB),
        cost_estimate=pl.CostEstimate(
            flops=10**9, bytes_accessed=7 * MIB, transcendentals=0
        ),
    )(received, token_rows, gain, pltpu.with_memory_space_constraint(place, pltpu.VMEM))
    exchanged = (experts, CAP * PARTS, PART)
    arrived = lax.all_to_all(
        outgoing.reshape(exchanged), ("ctx", "exp"), 0, 0, tiled=True
    ).reshape(slots * PARTS, PART)
    results = pl.pallas_call(
        expert_kernel,
        out_shape=jax.ShapeDtypeStruct((slots * PARTS, PART), BF16),
        in_specs=[in_vmem] * 3,
        out_specs=in_vmem,
        scratch_shapes=[pltpu.VMEM((slots, D), BF16), pltpu.VMEM((slots, 2 * EW), F32)],
        compiler_params=pltpu.CompilerParams(vmem_limit_bytes=10 * MIB),
        cost_estimate=pl.CostEstimate(
            flops=8 * 10**9, bytes_accessed=6 * MIB, transcendentals=3 * 10**5
        ),
    )(
        arrived,
        pltpu.with_memory_space_constraint(expand, pltpu.VMEM),
        pltpu.with_memory_space_constraint(reduce, pltpu.VMEM),
    )
    returned = lax.all_to_all(
        results.reshape(exchanged), ("ctx", "exp"), 0, 0, tiled=True
    ).reshape(slots * PARTS, PART)
    layer = call(
        combine_kernel,
        jax.ShapeDtypeStruct((rows, D), BF16),
        [],
        8,
        10**9,
        5 * MIB,
    )(returned, mix, stream)
    return jnp.swapaxes(layer.reshape(pairs, tokens.shape[0], D), 0, 1)


def solution(mesh):
    in_specs = (
        P(("ctx", "exp"), None, None),
        P("ctx", None, "exp"),
        P("ctx", None, None),
        P("ctx", None, None),
        P("exp", None),
        P(),
        P(("ctx", "exp"), None, None),
        P(("ctx", "exp"), None, None),
        P(("ctx", "exp"), None, None),
        P(("ctx", "exp"), None, None),
    )
    out_specs = P(("ctx", "exp"), None, None)
    return jax.shard_map(shards, mesh=mesh, in_specs=in_specs, out_specs=out_specs, check_vma=False)
```

```python
import functools

import jax
import jax.numpy as jnp
from jax import lax
from jax.experimental import pallas as pl
from jax.experimental.pallas import tpu as pltpu
from jax.sharding import PartitionSpec as P

D = 4096
HEADS = 32
KV_HEADS = 2
HEAD_DIM = 128
EW = 768
TOP = 8
CAP = 3
PARTS = 8
PART = D // PARTS
ALONE = 256
TILE = 16
LOG2E = 1.4426950408889634
F32 = jnp.float32
BF16 = jnp.bfloat16
MIB = 1 << 20


def contract(lhs, rhs, lhs_dim, rhs_dim):
    return lax.dot_general(
        lhs, rhs, (((lhs_dim,), (rhs_dim,)), ((), ())), preferred_element_type=F32
    )


def pieces(source, target, count, sem, first):
    size = source.shape[0] // count
    return [
        pltpu.make_async_copy(
            source.at[pl.ds(i * size, size), :],
            target.at[pl.ds(i * size, size), :],
            sem.at[first + i],
        )
        for i in range(count)
    ]


def pack_kernel(info_ref, weight_ref, query_ref, out_ref, flat_ref, buf_ref, query_buf, sem):
    depth = weight_ref.shape[0]
    width = out_ref.shape[1]
    extra = out_ref.shape[0] - depth
    length, pairs, local = query_ref.shape
    count = 8
    columns = weight_ref.at[:, pl.ds(pl.multiple_of(info_ref[0], PART), width)]
    query_copy = pltpu.make_async_copy(query_ref, query_buf, sem.at[0])
    query_copy.start()
    inward = pieces(columns, buf_ref.at[pl.ds(0, depth), :], count, sem, 1)
    outward = pieces(
        buf_ref.at[pl.ds(0, depth), :], out_ref.at[pl.ds(0, depth), :], count, sem, 1 + count
    )
    tail = pl.ds(depth, extra)
    outward.append(
        pltpu.make_async_copy(
            buf_ref.at[tail, :], out_ref.at[tail, :], sem.at[1 + 2 * count]
        )
    )
    for copy in inward:
        copy.start()
    query_copy.wait()
    lanes = width // HEAD_DIM
    for p in range(pairs):
        query = query_buf[:, p, :]
        flat_ref[:, p * local : (p + 1) * local] = query
        for h in range(local // HEAD_DIM):
            for r in range(length // TILE):
                slot = (p * local // HEAD_DIM + h) * (length // TILE) + r
                row = depth + slot // lanes * TILE
                at = slot % lanes * HEAD_DIM
                buf_ref[row : row + TILE, at : at + HEAD_DIM] = query[
                    r * TILE : (r + 1) * TILE, h * HEAD_DIM : (h + 1) * HEAD_DIM
                ]
    outward[count].start()
    for i in range(count):
        inward[i].wait()
        outward[i].start()
    for copy in outward:
        copy.wait()


def attend_kernel(
    info_ref,
    q0_ref,
    own_ref,
    near_ref,
    far_ref,
    weight_ref,
    side_ref,
    out_ref,
    score_ref,
    bias_ref,
    w0_ref,
    w1_ref,
    q1_ref,
    sem,
    *,
    pairs,
    heads,
):
    length = own_ref.shape[0]
    depth = w0_ref.shape[0]
    shared = w1_ref.shape[1]
    half = shared + ALONE
    copies = [
        pltpu.make_async_copy(
            side_ref.at[pl.ds(depth, q1_ref.shape[0]), :], q1_ref, sem.at[0]
        ),
        pltpu.make_async_copy(
            weight_ref.at[:, pl.ds(pl.multiple_of(info_ref[0], half), half)],
            w0_ref.at[:, pl.ds(0, half)],
            sem.at[1],
        ),
        pltpu.make_async_copy(
            weight_ref.at[:, pl.ds(pl.multiple_of(half - info_ref[0] + shared, ALONE), ALONE)],
            w0_ref.at[:, pl.ds(half, ALONE)],
            sem.at[2],
        ),
        pltpu.make_async_copy(side_ref.at[pl.ds(0, depth), :], w1_ref, sem.at[3]),
    ]
    moved = 1
    lanes = shared // HEAD_DIM
    for copy in copies:
        copy.start()
    rows = heads * length
    scale = HEAD_DIM ** (-0.5) * LOG2E
    later = lax.broadcasted_iota(jnp.int32, (rows, length), 1) > (
        lax.broadcasted_iota(jnp.int32, (rows, length), 0) % length
    )
    span = 8 * length
    chunks = [
        (ref, start) for ref in (near_ref, far_ref) for start in range(0, ref.shape[0], span)
    ]
    one = (lax.broadcasted_iota(jnp.int32, (rows, HEAD_DIM), 1) == 0).astype(BF16)
    for i in range(len(chunks)):
        for j in range(span // length):
            hidden = jnp.where(info_ref[1 + i * (span // length) + j] > 0, 0.0, -1e30)
            bias_ref[i, j * length : (j + 1) * length, :] = jnp.full(
                (length, HEAD_DIM), hidden, F32
            ).astype(BF16)
    groups = out_ref.shape[0]
    keep = length // groups
    stacked = []
    for q_ref in (q0_ref, q1_ref):
        if q_ref is q1_ref:
            for copy in copies[:moved]:
                copy.wait()
        attended = []
        for p in range(pairs):
            keys = slice(p * 2 * HEAD_DIM, (p * 2 + 1) * HEAD_DIM)
            values = slice((p * 2 + 1) * HEAD_DIM, (p * 2 + 2) * HEAD_DIM)
            blocks = []
            for head in range(p * heads, (p + 1) * heads):
                if q_ref is q0_ref:
                    blocks.append(q_ref[:, head * HEAD_DIM : (head + 1) * HEAD_DIM])
                    continue
                for slot in range(head * (length // TILE), (head + 1) * (length // TILE)):
                    row, at = slot // lanes * TILE, slot % lanes * HEAD_DIM
                    blocks.append(q_ref[row : row + TILE, at : at + HEAD_DIM])
            query = jnp.concatenate(blocks, axis=0)
            score = jnp.where(later, -1e30, contract(query, own_ref[:, keys], 1, 1))
            score_ref[:, :length] = score
            peak = score
            marked = jnp.concatenate([query, one], axis=1)
            for i, (ref, start) in enumerate(chunks):
                key = jnp.concatenate([ref[start : start + span, keys], bias_ref[i]], axis=1)
                score = contract(marked, key, 1, 1)
                at = length + i * span
                score_ref[:, at : at + span] = score
                for j in range(0, span, length):
                    peak = jnp.maximum(peak, score[:, j : j + length])
            peak = jnp.max(peak, axis=1, keepdims=True)
            weight = jnp.exp2((score_ref[:, :length] - peak) * scale)
            mass = weight
            acc = jnp.dot(weight.astype(BF16), own_ref[:, values], preferred_element_type=F32)
            for i, (ref, start) in enumerate(chunks):
                at = length + i * span
                weight = jnp.exp2((score_ref[:, at : at + span] - peak) * scale)
                for j in range(0, span, length):
                    mass = mass + weight[:, j : j + length]
                acc = acc + jnp.dot(
                    weight.astype(BF16),
                    ref[start : start + span, values],
                    preferred_element_type=F32,
                )
            acc = (acc / jnp.sum(mass, axis=1, keepdims=True)).astype(BF16)
            attended.append(
                jnp.concatenate(
                    [acc[h * length : (h + 1) * length] for h in range(heads)], axis=1
                )
            )
        stacked.append(jnp.concatenate(attended, axis=0))
    for copy in copies[moved:]:
        copy.wait()
    step = ALONE
    for n in range(0, half + ALONE, step):
        part = jnp.dot(stacked[0], w0_ref[:, n : n + step], preferred_element_type=F32)
        if n < shared:
            part = part + jnp.dot(
                stacked[1], w1_ref[:, n : n + step], preferred_element_type=F32
            )
        part = part.astype(BF16)
        for p in range(pairs):
            out_ref[:, p * keep : (p + 1) * keep, n : n + step] = part[
                p * length : (p + 1) * length
            ].reshape(groups, keep, step)


def prepare_kernel(routing_ref, gate_ref, place_ref, mix_ref):
    rows = routing_ref.shape[0]
    experts = place_ref.shape[0] // (CAP * PARTS)
    slots = place_ref.shape[0]
    width = PARTS * rows
    expert_iota = lax.broadcasted_iota(jnp.int32, (rows, experts), 1)
    named = jnp.zeros((rows, experts), F32)
    gates = jnp.zeros((rows, experts), F32)
    for k in range(TOP):
        hit = routing_ref[:, k : k + 1] == expert_iota
        named = jnp.where(hit, 1.0, named)
        gates = jnp.where(hit, gate_ref[:, k : k + 1], gates)
    lower = (
        lax.broadcasted_iota(jnp.int32, (rows, rows), 0)
        >= lax.broadcasted_iota(jnp.int32, (rows, rows), 1)
    ).astype(BF16)
    rank = named * jnp.dot(lower, named.astype(BF16), preferred_element_type=F32)
    spread = (
        lax.broadcasted_iota(jnp.int32, (rows, width), 0)
        == lax.broadcasted_iota(jnp.int32, (rows, width), 1) % rows
    ).astype(BF16)
    wide = contract(rank.astype(BF16), spread, 0, 0).astype(BF16)
    chunk = 768
    for s in range(0, slots, chunk):
        slot = s + lax.broadcasted_iota(jnp.int32, (chunk, experts), 0)
        owner = (
            slot // (CAP * PARTS) == lax.broadcasted_iota(jnp.int32, (chunk, experts), 1)
        ).astype(BF16)
        ranks = jnp.dot(owner, wide, preferred_element_type=F32)
        row = s + lax.broadcasted_iota(jnp.int32, (chunk, width), 0)
        col = lax.broadcasted_iota(jnp.int32, (chunk, width), 1)
        hit = (ranks == (row // PARTS % CAP + 1).astype(F32)) & (row % PARTS == col // rows)
        place_ref[s : s + chunk, :] = hit.astype(BF16)
        slot = s + lax.broadcasted_iota(jnp.int32, (experts, chunk), 1)
        owner = (
            slot // (CAP * PARTS) == lax.broadcasted_iota(jnp.int32, (experts, chunk), 0)
        ).astype(BF16)
        ranks = jnp.dot(rank.astype(BF16), owner, preferred_element_type=F32)
        value = jnp.dot(gates.astype(BF16), owner, preferred_element_type=F32)
        col = s + lax.broadcasted_iota(jnp.int32, (rows, chunk), 1)
        value = jnp.where(ranks == (col // PARTS % CAP + 1).astype(F32), value, 0.0)
        for c in range(PARTS):
            mix_ref[c * rows : (c + 1) * rows, s : s + chunk] = jnp.where(
                col % PARTS == c, value, 0.0
            ).astype(BF16)


def dispatch_kernel(
    part_ref, token_ref, gain_ref, place_ref, out_ref, stream_ref
):
    sources = part_ref.shape[0]
    rows = token_ref.shape[0]
    half = PARTS // 2
    square = jnp.zeros((rows, 1), F32)
    for c in range(PARTS):
        at = slice(c % half * PART, (c % half + 1) * PART)
        total = token_ref[:, c * PART : (c + 1) * PART].astype(F32)
        total = total + sum(
            part_ref[s, :, at].astype(F32) for s in range(c // half, sources, 2)
        )
        if c % half == half - 1:
            alone = sum(
                part_ref[s, :, D // 2 :].astype(F32)
                for s in range(1 - c // half, sources, 2)
            )
            total = jnp.concatenate(
                [total[:, : PART - ALONE], total[:, PART - ALONE :] + alone], axis=1
            )
        stream = total.astype(BF16)
        stream_ref[c * rows : (c + 1) * rows, :] = stream
        wide = stream.astype(F32)
        square = square + jnp.sum(wide * wide, axis=1, keepdims=True)
    factor = lax.rsqrt(square * (1.0 / D) + 1e-06)
    normed = jnp.concatenate(
        [
            (
                stream_ref[c * rows : (c + 1) * rows, :].astype(F32)
                * factor
                * gain_ref[:, c * PART : (c + 1) * PART].astype(F32)
            ).astype(BF16)
            for c in range(PARTS)
        ],
        axis=0,
    )
    step = 384
    for s in range(0, place_ref.shape[0], step):
        out_ref[s : s + step, :] = jnp.dot(
            place_ref[s : s + step, :], normed, preferred_element_type=F32
        ).astype(BF16)


def expert_kernel(x_ref, w1_ref, w2_ref, out_ref, rows_ref, gated_ref):
    slots = rows_ref.shape[0]
    group = 32
    size = group * PARTS
    left = lax.broadcasted_iota(jnp.int32, (size, size), 0)
    right = lax.broadcasted_iota(jnp.int32, (size, size), 1)
    gather = ((left % group) * PARTS + left // group == right).astype(BF16)
    scatter = ((right % group) * PARTS + right // group == left).astype(BF16)
    for g in range(slots // group):
        moved = jnp.dot(
            gather, x_ref[g * size : (g + 1) * size, :], preferred_element_type=F32
        ).astype(BF16)
        for c in range(PARTS):
            rows_ref[g * group : (g + 1) * group, c * PART : (c + 1) * PART] = moved[
                c * group : (c + 1) * group, :
            ]
    for c in range(PARTS):
        for n in range(0, 2 * EW, PART):
            part = jnp.dot(
                rows_ref[:, c * PART : (c + 1) * PART],
                w1_ref[c * PART : (c + 1) * PART, n : n + PART],
                preferred_element_type=F32,
            )
            if c == 0:
                gated_ref[:, n : n + PART] = part
            else:
                gated_ref[:, n : n + PART] += part
    gate = gated_ref[:, :EW]
    active = (gate / (1.0 + jnp.exp(-gate)) * gated_ref[:, EW:]).astype(BF16)
    for c in range(PARTS):
        rows_ref[:, c * PART : (c + 1) * PART] = jnp.dot(
            active, w2_ref[:, c * PART : (c + 1) * PART], preferred_element_type=F32
        ).astype(BF16)
    for g in range(slots // group):
        stacked = jnp.concatenate(
            [
                rows_ref[g * group : (g + 1) * group, c * PART : (c + 1) * PART]
                for c in range(PARTS)
            ],
            axis=0,
        )
        out_ref[g * size : (g + 1) * size, :] = jnp.dot(
            scatter, stacked, preferred_element_type=F32
        ).astype(BF16)


def combine_kernel(back_ref, mix_ref, stream_ref, out_ref):
    rows = out_ref.shape[0]
    mixture = jnp.dot(mix_ref[...], back_ref[...], preferred_element_type=F32)
    layer = (stream_ref[...].astype(F32) + mixture).astype(BF16)
    for c in range(PARTS):
        out_ref[:, c * PART : (c + 1) * PART] = layer[c * rows : (c + 1) * rows, :]


def call(kernel, outs, scratch, limit, flops, moved):
    return pl.pallas_call(
        kernel,
        out_shape=outs,
        scratch_shapes=scratch,
        compiler_params=pltpu.CompilerParams(vmem_limit_bytes=limit * MIB),
        cost_estimate=pl.CostEstimate(flops=flops, bytes_accessed=moved, transcendentals=0),
    )


def shards(
    tokens,
    queries,
    keys,
    values,
    output_weight,
    norm_gain,
    routing,
    gate_values,
    expand_weight,
    reduce_weight,
):
    length, pairs, local = queries.shape
    heads = local // HEAD_DIM
    context_size = lax.axis_size("ctx")
    expert_size = lax.axis_size("exp")
    experts = context_size * expert_size
    here = lax.axis_index("ctx")
    key_head = lax.axis_index("exp") * heads // (HEADS // KV_HEADS)
    rows = tokens.shape[0] * pairs
    slots = experts * CAP

    own = jnp.concatenate(
        [
            lax.dynamic_slice_in_dim(array, key_head * HEAD_DIM, HEAD_DIM, 2)
            for array in (keys, values)
        ],
        axis=2,
    ).reshape(length, pairs * 2 * HEAD_DIM)
    blocks = context_size // 2
    core = here % 2
    side = lax.axis_index("exp") % 2
    swap_core = [(c, c ^ 1) for c in range(context_size)]
    swap_side = [
        (c * expert_size + e, c * expert_size + (e ^ (1 + 2 * (c % 2))))
        for c in range(context_size)
        for e in range(expert_size)
    ]
    hbm_weight = pltpu.with_memory_space_constraint(output_weight, pltpu.HBM)
    half = D // 2
    in_vmem = pl.BlockSpec(memory_space=pltpu.VMEM)
    anywhere = pl.BlockSpec(memory_space=pl.ANY)
    in_smem = pl.BlockSpec(memory_space=pltpu.SMEM)
    in_hbm = pl.BlockSpec(memory_space=pltpu.HBM)
    shared = half - ALONE
    query_rows = -(-length * pairs * local // (shared * TILE)) * TILE
    packed_rows = local + query_rows
    sent, query = pl.pallas_call(
        pack_kernel,
        out_shape=(
            jax.ShapeDtypeStruct((packed_rows, shared), BF16),
            jax.ShapeDtypeStruct((length, pairs * local), BF16),
        ),
        in_specs=[in_smem, in_hbm, in_hbm],
        out_specs=(in_hbm, in_vmem),
        scratch_shapes=[
            pltpu.VMEM((packed_rows, shared), BF16),
            pltpu.VMEM(queries.shape, BF16),
            pltpu.SemaphoreType.DMA((18,)),
        ],
        compiler_params=pltpu.CompilerParams(vmem_limit_bytes=8 * MIB),
        cost_estimate=pl.CostEstimate(flops=0, bytes_accessed=5 * MIB, transcendentals=0),
    )(((1 - side) * half).astype(jnp.int32)[None], hbm_weight, pltpu.with_memory_space_constraint(queries, pltpu.HBM))
    from_side = lax.ppermute(sent, ("ctx", "exp"), swap_side)
    same = [[c for c in range(k, context_size, 2)] for k in range(2)]
    near = lax.all_to_all(
        jnp.broadcast_to(own[None], (blocks,) + own.shape),
        "ctx",
        0,
        0,
        axis_index_groups=same,
        tiled=True,
    )
    far = lax.ppermute(near, "ctx", swap_core)
    block = jnp.arange(blocks, dtype=jnp.int32) * 2
    order = jnp.concatenate([block + core, block + 1 - core])
    info = jnp.concatenate(
        [(side * half).astype(jnp.int32)[None], (order < here).astype(jnp.int32)]
    )
    def pair_major(array):
        return jnp.swapaxes(array, 0, 1).reshape(rows, array.shape[2])

    place, mix = call(
        prepare_kernel,
        (
            pltpu.VMEM((slots * PARTS, PARTS * rows), BF16),
            jax.ShapeDtypeStruct((PARTS * rows, slots * PARTS), BF16),
        ),
        [],
        8,
        10**9,
        3 * MIB,
    )(pair_major(routing), pair_major(gate_values))
    token_rows, gain = pair_major(tokens), norm_gain[None]
    info, place, mix, token_rows, gain = lax.optimization_barrier(
        (info, place, mix, token_rows, gain)
    )
    projected = pl.pallas_call(
        functools.partial(attend_kernel, pairs=pairs, heads=heads),
        out_shape=jax.ShapeDtypeStruct((expert_size, rows, half + ALONE), BF16),
        in_specs=[in_smem] + [in_vmem] * 4 + [in_hbm] * 2,
        out_specs=in_vmem,
        scratch_shapes=[
            pltpu.VMEM((heads * length, (context_size + 1) * length), F32),
            pltpu.VMEM((2, blocks * length, HEAD_DIM), BF16),
            pltpu.VMEM((local, half + ALONE), BF16),
            pltpu.VMEM((local, shared), BF16),
            pltpu.VMEM((query_rows, shared), BF16),
            pltpu.SemaphoreType.DMA((4,)),
        ],
        compiler_params=pltpu.CompilerParams(vmem_limit_bytes=22 * MIB),
        cost_estimate=pl.CostEstimate(
            flops=3 * 10**9, bytes_accessed=9 * MIB, transcendentals=4 * 10**6
        ),
    )(
        info,
        query,
        own,
        pltpu.with_memory_space_constraint(near.reshape(blocks * length, -1), pltpu.VMEM),
        pltpu.with_memory_space_constraint(far.reshape(blocks * length, -1), pltpu.VMEM),
        hbm_weight,
        pltpu.with_memory_space_constraint(from_side, pltpu.HBM),
    )

    projected, expand, reduce = lax.optimization_barrier(
        (projected, expand_weight[0], reduce_weight[0])
    )
    received = lax.all_to_all(projected, "exp", 0, 0, tiled=True)

    outgoing, stream = pl.pallas_call(
        dispatch_kernel,
        out_shape=(
            jax.ShapeDtypeStruct((slots * PARTS, PART), BF16),
            jax.ShapeDtypeStruct((PARTS * rows, PART), BF16),
        ),
        in_specs=[in_vmem] * 4,
        out_specs=(in_vmem, in_vmem),
        compiler_params=pltpu.CompilerParams(vmem_limit_bytes=8 * MIB),
        cost_estimate=pl.CostEstimate(
            flops=10**9, bytes_accessed=7 * MIB, transcendentals=0
        ),
    )(received, token_rows, gain, pltpu.with_memory_space_constraint(place, pltpu.VMEM))
    exchanged = (experts, CAP * PARTS, PART)
    arrived = lax.all_to_all(
        outgoing.reshape(exchanged), ("ctx", "exp"), 0, 0, tiled=True
    ).reshape(slots * PARTS, PART)
    results = pl.pallas_call(
        expert_kernel,
        out_shape=jax.ShapeDtypeStruct((slots * PARTS, PART), BF16),
        in_specs=[in_vmem] * 3,
        out_specs=in_vmem,
        scratch_shapes=[pltpu.VMEM((slots, D), BF16), pltpu.VMEM((slots, 2 * EW), F32)],
        compiler_params=pltpu.CompilerParams(vmem_limit_bytes=10 * MIB),
        cost_estimate=pl.CostEstimate(
            flops=8 * 10**9, bytes_accessed=6 * MIB, transcendentals=3 * 10**5
        ),
    )(
        arrived,
        pltpu.with_memory_space_constraint(expand, pltpu.VMEM),
        pltpu.with_memory_space_constraint(reduce, pltpu.VMEM),
    )
    returned = lax.all_to_all(
        results.reshape(exchanged), ("ctx", "exp"), 0, 0, tiled=True
    ).reshape(slots * PARTS, PART)
    layer = call(
        combine_kernel,
        jax.ShapeDtypeStruct((rows, D), BF16),
        [],
        8,
        10**9,
        5 * MIB,
    )(returned, mix, stream)
    return jnp.swapaxes(layer.reshape(pairs, tokens.shape[0], D), 0, 1)


def solution(mesh):
    in_specs = (
        P(("ctx", "exp"), None, None),
        P("ctx", None, "exp"),
        P("ctx", None, None),
        P("ctx", None, None),
        P("exp", None),
        P(),
        P(("ctx", "exp"), None, None),
        P(("ctx", "exp"), None, None),
        P(("ctx", "exp"), None, None),
        P(("ctx", "exp"), None, None),
    )
    out_specs = P(("ctx", "exp"), None, None)
    return jax.shard_map(shards, mesh=mesh, in_specs=in_specs, out_specs=out_specs, check_vma=False)
```

```python
import functools

import jax
import jax.numpy as jnp
from jax import lax
from jax.experimental import pallas as pl
from jax.experimental.pallas import tpu as pltpu
from jax.sharding import PartitionSpec as P

D = 4096
HEADS = 32
KV_HEADS = 2
HEAD_DIM = 128
EW = 768
TOP = 8
CAP = 3
PARTS = 8
PART = D // PARTS
ALONE = 256
TILE = 16
LOG2E = 1.4426950408889634
F32 = jnp.float32
BF16 = jnp.bfloat16
MIB = 1 << 20


def contract(lhs, rhs, lhs_dim, rhs_dim):
    return lax.dot_general(
        lhs, rhs, (((lhs_dim,), (rhs_dim,)), ((), ())), preferred_element_type=F32
    )


def pieces(source, target, count, sem, first):
    size = source.shape[0] // count
    return [
        pltpu.make_async_copy(
            source.at[pl.ds(i * size, size), :],
            target.at[pl.ds(i * size, size), :],
            sem.at[first + i],
        )
        for i in range(count)
    ]


def pack_kernel(info_ref, weight_ref, query_ref, out_ref, flat_ref, buf_ref, query_buf, sem):
    depth = weight_ref.shape[0]
    width = out_ref.shape[1]
    extra = out_ref.shape[0] - depth
    length, pairs, local = query_ref.shape
    count = 8
    columns = weight_ref.at[:, pl.ds(pl.multiple_of(info_ref[0], PART), width)]
    query_copy = pltpu.make_async_copy(query_ref, query_buf, sem.at[0])
    query_copy.start()
    inward = pieces(columns, buf_ref.at[pl.ds(0, depth), :], count, sem, 1)
    outward = pieces(
        buf_ref.at[pl.ds(0, depth), :], out_ref.at[pl.ds(0, depth), :], count, sem, 1 + count
    )
    tail = pl.ds(depth, extra)
    outward.append(
        pltpu.make_async_copy(
            buf_ref.at[tail, :], out_ref.at[tail, :], sem.at[1 + 2 * count]
        )
    )
    for copy in inward:
        copy.start()
    for i in range(count):
        inward[i].wait()
        outward[i].start()
    query_copy.wait()
    lanes = width // HEAD_DIM
    for p in range(pairs):
        query = query_buf[:, p, :]
        flat_ref[:, p * local : (p + 1) * local] = query
        for h in range(local // HEAD_DIM):
            for r in range(length // TILE):
                slot = (p * local // HEAD_DIM + h) * (length // TILE) + r
                row = depth + slot // lanes * TILE
                at = slot % lanes * HEAD_DIM
                buf_ref[row : row + TILE, at : at + HEAD_DIM] = query[
                    r * TILE : (r + 1) * TILE, h * HEAD_DIM : (h + 1) * HEAD_DIM
                ]
    outward[count].start()
    for copy in outward:
        copy.wait()


def attend_kernel(
    info_ref,
    q0_ref,
    own_ref,
    near_ref,
    far_ref,
    weight_ref,
    side_ref,
    out_ref,
    score_ref,
    bias_ref,
    w0_ref,
    w1_ref,
    q1_ref,
    sem,
    *,
    pairs,
    heads,
):
    length = own_ref.shape[0]
    depth = w0_ref.shape[0]
    shared = w1_ref.shape[1]
    half = shared + ALONE
    copies = [
        pltpu.make_async_copy(
            side_ref.at[pl.ds(depth, q1_ref.shape[0]), :], q1_ref, sem.at[0]
        ),
        pltpu.make_async_copy(
            weight_ref.at[:, pl.ds(pl.multiple_of(info_ref[0], half), half)],
            w0_ref.at[:, pl.ds(0, half)],
            sem.at[1],
        ),
        pltpu.make_async_copy(
            weight_ref.at[:, pl.ds(pl.multiple_of(half - info_ref[0] + shared, ALONE), ALONE)],
            w0_ref.at[:, pl.ds(half, ALONE)],
            sem.at[2],
        ),
        pltpu.make_async_copy(side_ref.at[pl.ds(0, depth), :], w1_ref, sem.at[3]),
    ]
    moved = 1
    lanes = shared // HEAD_DIM
    for copy in copies:
        copy.start()
    rows = heads * length
    scale = HEAD_DIM ** (-0.5) * LOG2E
    later = lax.broadcasted_iota(jnp.int32, (rows, length), 1) > (
        lax.broadcasted_iota(jnp.int32, (rows, length), 0) % length
    )
    span = 8 * length
    chunks = [
        (ref, start) for ref in (near_ref, far_ref) for start in range(0, ref.shape[0], span)
    ]
    one = (lax.broadcasted_iota(jnp.int32, (rows, HEAD_DIM), 1) == 0).astype(BF16)
    for i in range(len(chunks)):
        for j in range(span // length):
            hidden = jnp.where(info_ref[1 + i * (span // length) + j] > 0, 0.0, -1e30)
            bias_ref[i, j * length : (j + 1) * length, :] = jnp.full(
                (length, HEAD_DIM), hidden, F32
            ).astype(BF16)
    groups = out_ref.shape[0]
    keep = length // groups
    stacked = []
    for q_ref in (q0_ref, q1_ref):
        if q_ref is q1_ref:
            for copy in copies[:moved]:
                copy.wait()
        attended = []
        for p in range(pairs):
            keys = slice(p * 2 * HEAD_DIM, (p * 2 + 1) * HEAD_DIM)
            values = slice((p * 2 + 1) * HEAD_DIM, (p * 2 + 2) * HEAD_DIM)
            blocks = []
            for head in range(p * heads, (p + 1) * heads):
                if q_ref is q0_ref:
                    blocks.append(q_ref[:, head * HEAD_DIM : (head + 1) * HEAD_DIM])
                    continue
                for slot in range(head * (length // TILE), (head + 1) * (length // TILE)):
                    row, at = slot // lanes * TILE, slot % lanes * HEAD_DIM
                    blocks.append(q_ref[row : row + TILE, at : at + HEAD_DIM])
            query = jnp.concatenate(blocks, axis=0)
            score = jnp.where(later, -1e30, contract(query, own_ref[:, keys], 1, 1))
            score_ref[:, :length] = score
            peak = score
            marked = jnp.concatenate([query, one], axis=1)
            for i, (ref, start) in enumerate(chunks):
                key = jnp.concatenate([ref[start : start + span, keys], bias_ref[i]], axis=1)
                score = contract(marked, key, 1, 1)
                at = length + i * span
                score_ref[:, at : at + span] = score
                for j in range(0, span, length):
                    peak = jnp.maximum(peak, score[:, j : j + length])
            peak = jnp.max(peak, axis=1, keepdims=True)
            weight = jnp.exp2((score_ref[:, :length] - peak) * scale)
            mass = weight
            acc = jnp.dot(weight.astype(BF16), own_ref[:, values], preferred_element_type=F32)
            for i, (ref, start) in enumerate(chunks):
                at = length + i * span
                weight = jnp.exp2((score_ref[:, at : at + span] - peak) * scale)
                for j in range(0, span, length):
                    mass = mass + weight[:, j : j + length]
                acc = acc + jnp.dot(
                    weight.astype(BF16),
                    ref[start : start + span, values],
                    preferred_element_type=F32,
                )
            acc = (acc / jnp.sum(mass, axis=1, keepdims=True)).astype(BF16)
            attended.append(
                jnp.concatenate(
                    [acc[h * length : (h + 1) * length] for h in range(heads)], axis=1
                )
            )
        stacked.append(jnp.concatenate(attended, axis=0))
    for copy in copies[moved:]:
        copy.wait()
    step = ALONE
    for n in range(0, half + ALONE, step):
        part = jnp.dot(stacked[0], w0_ref[:, n : n + step], preferred_element_type=F32)
        if n < shared:
            part = part + jnp.dot(
                stacked[1], w1_ref[:, n : n + step], preferred_element_type=F32
            )
        part = part.astype(BF16)
        for p in range(pairs):
            out_ref[:, p * keep : (p + 1) * keep, n : n + step] = part[
                p * length : (p + 1) * length
            ].reshape(groups, keep, step)


def prepare_kernel(routing_ref, gate_ref, place_ref, mix_ref):
    rows = routing_ref.shape[0]
    experts = place_ref.shape[0] // (CAP * PARTS)
    slots = place_ref.shape[0]
    width = PARTS * rows
    expert_iota = lax.broadcasted_iota(jnp.int32, (rows, experts), 1)
    named = jnp.zeros((rows, experts), F32)
    gates = jnp.zeros((rows, experts), F32)
    for k in range(TOP):
        hit = routing_ref[:, k : k + 1] == expert_iota
        named = jnp.where(hit, 1.0, named)
        gates = jnp.where(hit, gate_ref[:, k : k + 1], gates)
    lower = (
        lax.broadcasted_iota(jnp.int32, (rows, rows), 0)
        >= lax.broadcasted_iota(jnp.int32, (rows, rows), 1)
    ).astype(BF16)
    rank = named * jnp.dot(lower, named.astype(BF16), preferred_element_type=F32)
    spread = (
        lax.broadcasted_iota(jnp.int32, (rows, width), 0)
        == lax.broadcasted_iota(jnp.int32, (rows, width), 1) % rows
    ).astype(BF16)
    wide = contract(rank.astype(BF16), spread, 0, 0).astype(BF16)
    chunk = 768
    for s in range(0, slots, chunk):
        row = s + lax.broadcasted_iota(jnp.int32, (chunk, 1), 0)
        expert = row // (CAP * PARTS)
        owner = (expert == lax.broadcasted_iota(jnp.int32, (chunk, experts), 1)).astype(BF16)
        ranks = jnp.dot(owner, wide, preferred_element_type=F32)
        part = lax.broadcasted_iota(jnp.int32, (chunk, width), 1) // rows
        hit = (ranks == (row // PARTS - CAP * expert + 1).astype(F32)) & (row % PARTS == part)
        place_ref[s : s + chunk, :] = hit.astype(BF16)
        col = s + lax.broadcasted_iota(jnp.int32, (1, chunk), 1)
        expert = col // (CAP * PARTS)
        owner = (expert == lax.broadcasted_iota(jnp.int32, (experts, chunk), 0)).astype(BF16)
        ranks = jnp.dot(rank.astype(BF16), owner, preferred_element_type=F32)
        value = jnp.dot(gates.astype(BF16), owner, preferred_element_type=F32)
        value = jnp.where(ranks == (col // PARTS - CAP * expert + 1).astype(F32), value, 0.0)
        for c in range(PARTS):
            mix_ref[c * rows : (c + 1) * rows, s : s + chunk] = jnp.where(
                col % PARTS == c, value, 0.0
            ).astype(BF16)


def dispatch_kernel(
    part_ref, token_ref, gain_ref, place_ref, out_ref, stream_ref
):
    sources = part_ref.shape[0]
    rows = token_ref.shape[0]
    half = PARTS // 2
    square = jnp.zeros((rows, 1), F32)
    for c in range(PARTS):
        at = slice(c % half * PART, (c % half + 1) * PART)
        total = token_ref[:, c * PART : (c + 1) * PART].astype(F32)
        total = total + sum(
            part_ref[s, :, at].astype(F32) for s in range(c // half, sources, 2)
        )
        if c % half == half - 1:
            alone = sum(
                part_ref[s, :, D // 2 :].astype(F32)
                for s in range(1 - c // half, sources, 2)
            )
            total = jnp.concatenate(
                [total[:, : PART - ALONE], total[:, PART - ALONE :] + alone], axis=1
            )
        stream = total.astype(BF16)
        stream_ref[c * rows : (c + 1) * rows, :] = stream
        wide = stream.astype(F32)
        square = square + jnp.sum(wide * wide, axis=1, keepdims=True)
    factor = lax.rsqrt(square * (1.0 / D) + 1e-06)
    normed = jnp.concatenate(
        [
            (
                stream_ref[c * rows : (c + 1) * rows, :].astype(F32)
                * factor
                * gain_ref[:, c * PART : (c + 1) * PART].astype(F32)
            ).astype(BF16)
            for c in range(PARTS)
        ],
        axis=0,
    )
    step = 384
    for s in range(0, place_ref.shape[0], step):
        out_ref[s : s + step, :] = jnp.dot(
            place_ref[s : s + step, :], normed, preferred_element_type=F32
        ).astype(BF16)


def expert_kernel(x_ref, w1_ref, w2_ref, out_ref, rows_ref, gated_ref):
    slots = rows_ref.shape[0]
    group = 32
    size = group * PARTS
    left = lax.broadcasted_iota(jnp.int32, (size, size), 0)
    right = lax.broadcasted_iota(jnp.int32, (size, size), 1)
    gather = ((left % group) * PARTS + left // group == right).astype(BF16)
    scatter = ((right % group) * PARTS + right // group == left).astype(BF16)
    for g in range(slots // group):
        moved = jnp.dot(
            gather, x_ref[g * size : (g + 1) * size, :], preferred_element_type=F32
        ).astype(BF16)
        for c in range(PARTS):
            rows_ref[g * group : (g + 1) * group, c * PART : (c + 1) * PART] = moved[
                c * group : (c + 1) * group, :
            ]
    for n in range(0, 2 * EW, PART):
        gated_ref[:, n : n + PART] = jnp.dot(
            rows_ref[...], w1_ref[:, n : n + PART], preferred_element_type=F32
        )
    gate = gated_ref[:, :EW]
    active = (gate / (1.0 + jnp.exp(-gate)) * gated_ref[:, EW:]).astype(BF16)
    for c in range(PARTS):
        rows_ref[:, c * PART : (c + 1) * PART] = jnp.dot(
            active, w2_ref[:, c * PART : (c + 1) * PART], preferred_element_type=F32
        ).astype(BF16)
    for g in range(slots // group):
        stacked = jnp.concatenate(
            [
                rows_ref[g * group : (g + 1) * group, c * PART : (c + 1) * PART]
                for c in range(PARTS)
            ],
            axis=0,
        )
        out_ref[g * size : (g + 1) * size, :] = jnp.dot(
            scatter, stacked, preferred_element_type=F32
        ).astype(BF16)


def combine_kernel(back_ref, mix_ref, stream_ref, out_ref):
    rows = out_ref.shape[0]
    mixture = jnp.dot(mix_ref[...], back_ref[...], preferred_element_type=F32)
    layer = (stream_ref[...].astype(F32) + mixture).astype(BF16)
    for c in range(PARTS):
        out_ref[:, c * PART : (c + 1) * PART] = layer[c * rows : (c + 1) * rows, :]


def call(kernel, outs, scratch, limit, flops, moved):
    return pl.pallas_call(
        kernel,
        out_shape=outs,
        scratch_shapes=scratch,
        compiler_params=pltpu.CompilerParams(vmem_limit_bytes=limit * MIB),
        cost_estimate=pl.CostEstimate(flops=flops, bytes_accessed=moved, transcendentals=0),
    )


def shards(
    tokens,
    queries,
    keys,
    values,
    output_weight,
    norm_gain,
    routing,
    gate_values,
    expand_weight,
    reduce_weight,
):
    length, pairs, local = queries.shape
    heads = local // HEAD_DIM
    context_size = lax.axis_size("ctx")
    expert_size = lax.axis_size("exp")
    experts = context_size * expert_size
    here = lax.axis_index("ctx")
    key_head = lax.axis_index("exp") * heads // (HEADS // KV_HEADS)
    rows = tokens.shape[0] * pairs
    slots = experts * CAP

    own = jnp.concatenate(
        [
            lax.dynamic_slice_in_dim(array, key_head * HEAD_DIM, HEAD_DIM, 2)
            for array in (keys, values)
        ],
        axis=2,
    ).reshape(length, pairs * 2 * HEAD_DIM)
    blocks = context_size // 2
    core = here % 2
    side = lax.axis_index("exp") % 2
    swap_core = [(c, c ^ 1) for c in range(context_size)]
    swap_side = [
        (c * expert_size + e, c * expert_size + (e ^ (1 + 2 * (c % 2))))
        for c in range(context_size)
        for e in range(expert_size)
    ]
    hbm_weight = pltpu.with_memory_space_constraint(output_weight, pltpu.HBM)
    half = D // 2
    in_vmem = pl.BlockSpec(memory_space=pltpu.VMEM)
    anywhere = pl.BlockSpec(memory_space=pl.ANY)
    in_smem = pl.BlockSpec(memory_space=pltpu.SMEM)
    in_hbm = pl.BlockSpec(memory_space=pltpu.HBM)
    shared = half - ALONE
    query_rows = -(-length * pairs * local // (shared * TILE)) * TILE
    packed_rows = local + query_rows
    sent, query = pl.pallas_call(
        pack_kernel,
        out_shape=(
            jax.ShapeDtypeStruct((packed_rows, shared), BF16),
            jax.ShapeDtypeStruct((length, pairs * local), BF16),
        ),
        in_specs=[in_smem, in_hbm, in_hbm],
        out_specs=(in_hbm, in_vmem),
        scratch_shapes=[
            pltpu.VMEM((packed_rows, shared), BF16),
            pltpu.VMEM(queries.shape, BF16),
            pltpu.SemaphoreType.DMA((18,)),
        ],
        compiler_params=pltpu.CompilerParams(vmem_limit_bytes=8 * MIB),
        cost_estimate=pl.CostEstimate(flops=0, bytes_accessed=5 * MIB, transcendentals=0),
    )(((1 - side) * half).astype(jnp.int32)[None], hbm_weight, pltpu.with_memory_space_constraint(queries, pltpu.HBM))
    from_side = lax.ppermute(sent, ("ctx", "exp"), swap_side)
    same = [[c for c in range(k, context_size, 2)] for k in range(2)]
    near = lax.all_to_all(
        jnp.broadcast_to(own[None], (blocks,) + own.shape),
        "ctx",
        0,
        0,
        axis_index_groups=same,
        tiled=True,
    )
    far = lax.ppermute(near, "ctx", swap_core)
    block = jnp.arange(blocks, dtype=jnp.int32) * 2
    order = jnp.concatenate([block + core, block + 1 - core])
    info = jnp.concatenate(
        [(side * half).astype(jnp.int32)[None], (order < here).astype(jnp.int32)]
    )
    def pair_major(array):
        return jnp.swapaxes(array, 0, 1).reshape(rows, array.shape[2])

    place, mix = call(
        prepare_kernel,
        (
            pltpu.VMEM((slots * PARTS, PARTS * rows), BF16),
            jax.ShapeDtypeStruct((PARTS * rows, slots * PARTS), BF16),
        ),
        [],
        8,
        10**9,
        3 * MIB,
    )(pair_major(routing), pair_major(gate_values))
    token_rows, gain = pair_major(tokens), norm_gain[None]
    info, place, mix, token_rows, gain = lax.optimization_barrier(
        (info, place, mix, token_rows, gain)
    )
    projected = pl.pallas_call(
        functools.partial(attend_kernel, pairs=pairs, heads=heads),
        out_shape=jax.ShapeDtypeStruct((expert_size, rows, half + ALONE), BF16),
        in_specs=[in_smem] + [in_vmem] * 4 + [in_hbm] * 2,
        out_specs=in_vmem,
        scratch_shapes=[
            pltpu.VMEM((heads * length, (context_size + 1) * length), F32),
            pltpu.VMEM((2, blocks * length, HEAD_DIM), BF16),
            pltpu.VMEM((local, half + ALONE), BF16),
            pltpu.VMEM((local, shared), BF16),
            pltpu.VMEM((query_rows, shared), BF16),
            pltpu.SemaphoreType.DMA((4,)),
        ],
        compiler_params=pltpu.CompilerParams(vmem_limit_bytes=22 * MIB),
        cost_estimate=pl.CostEstimate(
            flops=3 * 10**9, bytes_accessed=9 * MIB, transcendentals=4 * 10**6
        ),
    )(
        info,
        query,
        own,
        pltpu.with_memory_space_constraint(near.reshape(blocks * length, -1), pltpu.VMEM),
        pltpu.with_memory_space_constraint(far.reshape(blocks * length, -1), pltpu.VMEM),
        hbm_weight,
        pltpu.with_memory_space_constraint(from_side, pltpu.HBM),
    )

    projected, expand, reduce = lax.optimization_barrier(
        (projected, expand_weight[0], reduce_weight[0])
    )
    received = lax.all_to_all(projected, "exp", 0, 0, tiled=True)

    outgoing, stream = pl.pallas_call(
        dispatch_kernel,
        out_shape=(
            jax.ShapeDtypeStruct((slots * PARTS, PART), BF16),
            jax.ShapeDtypeStruct((PARTS * rows, PART), BF16),
        ),
        in_specs=[in_vmem] * 4,
        out_specs=(in_vmem, in_vmem),
        compiler_params=pltpu.CompilerParams(vmem_limit_bytes=8 * MIB),
        cost_estimate=pl.CostEstimate(
            flops=10**9, bytes_accessed=7 * MIB, transcendentals=0
        ),
    )(received, token_rows, gain, pltpu.with_memory_space_constraint(place, pltpu.VMEM))
    exchanged = (experts, CAP * PARTS, PART)
    arrived = lax.all_to_all(
        outgoing.reshape(exchanged), ("ctx", "exp"), 0, 0, tiled=True
    ).reshape(slots * PARTS, PART)
    results = pl.pallas_call(
        expert_kernel,
        out_shape=jax.ShapeDtypeStruct((slots * PARTS, PART), BF16),
        in_specs=[in_vmem] * 3,
        out_specs=in_vmem,
        scratch_shapes=[pltpu.VMEM((slots, D), BF16), pltpu.VMEM((slots, 2 * EW), F32)],
        compiler_params=pltpu.CompilerParams(vmem_limit_bytes=10 * MIB),
        cost_estimate=pl.CostEstimate(
            flops=8 * 10**9, bytes_accessed=6 * MIB, transcendentals=3 * 10**5
        ),
    )(
        arrived,
        pltpu.with_memory_space_constraint(expand, pltpu.VMEM),
        pltpu.with_memory_space_constraint(reduce, pltpu.VMEM),
    )
    returned = lax.all_to_all(
        results.reshape(exchanged), ("ctx", "exp"), 0, 0, tiled=True
    ).reshape(slots * PARTS, PART)
    layer = call(
        combine_kernel,
        jax.ShapeDtypeStruct((rows, D), BF16),
        [],
        8,
        10**9,
        5 * MIB,
    )(returned, mix, stream)
    return jnp.swapaxes(layer.reshape(pairs, tokens.shape[0], D), 0, 1)


def solution(mesh):
    in_specs = (
        P(("ctx", "exp"), None, None),
        P("ctx", None, "exp"),
        P("ctx", None, None),
        P("ctx", None, None),
        P("exp", None),
        P(),
        P(("ctx", "exp"), None, None),
        P(("ctx", "exp"), None, None),
        P(("ctx", "exp"), None, None),
        P(("ctx", "exp"), None, None),
    )
    out_specs = P(("ctx", "exp"), None, None)
    return jax.shard_map(shards, mesh=mesh, in_specs=in_specs, out_specs=out_specs, check_vma=False)
```
